128 devices in a mesh: gx: 16 (over x, y), gy: 8 (over z, core).
Axes of the slice: x: 4, y: 4, z: 4, core: 2. Of those that a mesh axis runs over, the one named last changes fastest.
Arguments:
- state: float32 [512, 256, 2048], P('gx', 'gy'), may hold values from 0.1 to 4
- lat_coef: float32 [512, 256], P('gx', 'gy'), may hold values from 0.05 to 0.2
- diffusion: float32 [512, 256, 64], P('gx', 'gy'), may hold values from 0.05 to 1
- layer_count: int32 [512, 256], P('gx', 'gy'), may hold values from 32 to 64
- species_scale: float32 [32], replicated, may hold values from 0.1 to 10
- stream: float32 [524288, 32], P(('gx', 'gy')), may hold values from 0.1 to 4
- reach_owner: int32 [524288, 1], P(('gx', 'gy')), may hold values from 0 to 127; in each aligned block of 4096 rows (0 to 4095, 4096 to 8191, ...) at most 64 rows name the same one
- reach_local: int32 [524288], P(('gx', 'gy')), may hold values from 0 to 1023
- exch_coef: float32 [524288], P(('gx', 'gy')), may hold values from 0.2 to 1
- rate_left: float32 [32, 64], replicated, may hold values from -1 to 1
- rate_right: float32 [32, 64], replicated, may hold values from -1 to 1
- stoich: float32 [64, 32], replicated, may hold values from -0.75 to 0.75
Outputs:
- state_out: float32 [512, 256, 2048], P('gx', 'gy')
- stream_out: float32 [524288, 32], P(('gx', 'gy'))
The draws below stay inside these ranges and needn't reach their ends.
Inputs may be any that keep to these rules, and one draw needn't show every extreme that they name: `reach_owner`: in the nodes of one device at most 64 have the same owner, and some owner gets exactly 64.
All inputs are finite; a program needn't handle non-finite values.
Results may differ from the reference program's by a relative error of at most 0.0003.
Values sent between devices are 32-bit elements; how exact they have to be, the bound alone decides.
A program may use at most 192 MiB of HBM per device.

```python
import math
import jax
import jax.numpy as jnp
import numpy as np
from jax import lax

CX = 32
CY = 32
LAYERS = 64
SPECIES = 32
REACTIONS = 64
NODES_DEV = 4096
CAP = 64
NX = 512
NY = 256
NODES = 524288
N_GY = 8
DEVICES = 128


def with_ends(array, rng, low, largest):
    extent = array.shape
    spot = [jax.random.randint(jax.random.fold_in(rng, axis), (), 0, extent[axis]) for axis in range(len(extent))]
    array = array.at[tuple(spot)].set(low)
    longest = extent.index(max(extent))
    spot[longest] = (spot[longest] + 1) % extent[longest]
    return array.at[tuple(spot)].set(largest)


def level_of(key, extent, shards, low, high):
    loudness = 1.0
    for axis_at, parts in shards:
        heights = jax.random.uniform(jax.random.fold_in(jax.random.fold_in(key, 6), axis_at), (parts,), jnp.float32, low / len(shards), high / len(shards))
        loudness = loudness * jnp.repeat(jnp.exp(heights), extent[axis_at] // parts).reshape((-1,) + (1,) * (len(extent) - 1 - axis_at))
    return loudness


def assign_block(stream_key, own, number, rows, count, top, reach, slope):
    sequence = jax.random.permutation(stream_key, count)
    crowded, common = shares(count, rows * top, reach, slope, True), shares(count, rows * top, reach, slope, False)
    places = jnp.arange(count)

    def named(sizes, rotation):
        used = int((sizes > 0).sum())
        fixed = max(1, used // 4)
        shifted = fixed + (places - fixed + rotation * (used - fixed)) % max(1, count - fixed)
        return jnp.zeros((count,), jnp.int32).at[sequence[jnp.where(places < fixed, places, shifted)]].set(jnp.asarray(sizes, jnp.int32))

    sizes = jnp.where(number % 4 == 0, named(crowded, number // 4), named(common, number - number // 4 - 1))
    mixed = jax.random.permutation(jax.random.fold_in(own, 3), count)
    giver, sink = mixed[0:count // 2 * 2:2], mixed[1:count // 2 * 2:2]
    slack = jnp.minimum(sizes[giver] - 1, reach - sizes[sink]) // 2
    slack = jnp.where((giver == sequence[0]) | (sink == sequence[0]) | (sizes[sink] == 0), 0, jnp.maximum(slack, 0))
    shifted = jax.random.randint(jax.random.fold_in(own, 4), (count // 2,), 0, 1 << 20) % (slack + 1)
    sizes = sizes.at[giver].add(-shifted).at[sink].add(shifted)
    members = jnp.searchsorted(jnp.cumsum(sizes), jnp.arange(rows * top), side="right").astype(jnp.int32)
    table = members.reshape(top, rows).T
    table = table[jax.random.permutation(jax.random.fold_in(own, 1), rows)]
    rotation = jax.random.randint(jax.random.fold_in(own, 2), (rows, 1), 0, top)
    return jnp.take_along_axis(table, (jnp.arange(top)[None, :] + rotation) % top, axis=1)


def shares(count, total, most, slope, full):
    weights = [(1 << 20) // math.isqrt(rank ** slope) + 1 for rank in range(1, count + 1)]
    largest = most if full else min(most, max(-(-total // count), total * weights[0] // sum(weights)))
    least = 1 if total - largest >= count - 1 else 0
    holding, spare = [largest] + [least] * (count - 1), total - largest - least * (count - 1)
    while spare > 0:
        movable = [i for i in range(1, count) if holding[i] < largest] or [i for i in range(1, count) if holding[i] < most]
        mass, left = sum([weights[i] for i in movable]), spare
        for i in movable:
            extra = min(most - holding[i], max(1, left * weights[i] // mass), spare)
            holding[i] = holding[i] + extra
            spare = spare - extra
    return np.array(holding)


def bell_draw(own_key, dims, deviation, reach, kind=jnp.bfloat16):
    return jnp.clip(deviation * jax.random.normal(own_key, dims, jnp.float32), -reach, reach).astype(kind)


def setup_inputs(seed: int = 0) -> dict:
    key_of = jax.random.split(jax.random.key(seed), 13)
    state = jnp.clip(jnp.exp(math.log(4.0) - 3.6888794 * jax.random.uniform(key_of[0], (NX, NY, LAYERS * SPECIES), jnp.float32) ** level_of(key_of[0], (NX, NY, LAYERS * SPECIES), ((0, 16), (1, 8)), -0.2, 0.2)), 0.1, 4.0)
    lat_coef = jnp.clip(0.05 + 0.15 * jax.random.uniform(key_of[1], (NX, NY), jnp.float32) ** level_of(key_of[1], (NX, NY), ((0, 16), (1, 8)), -0.2, 0.2), 0.05, 0.2)
    diffusion = jnp.clip(jnp.exp(math.log(1.0) - 2.9957323 * jax.random.uniform(key_of[2], (NX, NY, LAYERS), jnp.float32) ** level_of(key_of[2], (NX, NY, LAYERS), ((0, 16), (1, 8)), -0.2, 0.2)), 0.05, 1.0)
    layer_count = with_ends(jax.random.randint(key_of[3], (NX, NY), LAYERS // 2, LAYERS + 1), jax.random.fold_in(key_of[3], 1), LAYERS // 2, LAYERS).astype(jnp.int32)
    species_scale = jnp.clip(jnp.exp(jax.random.uniform(key_of[4], (SPECIES,), jnp.float32, math.log(0.1), math.log(10.0))), 0.1, 10.0)
    stream = jnp.clip(jnp.exp(math.log(4.0) - 3.6888794 * jax.random.uniform(key_of[5], (NODES, SPECIES), jnp.float32) ** level_of(key_of[5], (NODES, SPECIES), ((0, 128),), -0.2, 0.2)), 0.1, 4.0)
    reach_owner_keys = jax.random.split(jax.random.fold_in(key_of[6], 1), NODES // NODES_DEV)
    reach_owner_turns = jax.random.permutation(jax.random.fold_in(key_of[6], 3), NODES // NODES_DEV)
    reach_owner = jax.vmap(lambda own, number: assign_block(jax.random.fold_in(key_of[6], 2), own, number, NODES_DEV, DEVICES, 1, CAP, 2))(reach_owner_keys, reach_owner_turns).reshape((NODES, 1))
    reach_local = with_ends(jax.random.randint(key_of[7], (NODES,), 0, CX * CY), jax.random.fold_in(key_of[7], 1), 0, (CX * CY) - 1).astype(jnp.int32)
    exch_coef = jnp.clip(jnp.exp(math.log(1.0) - 1.609438 * jax.random.uniform(key_of[8], (NODES,), jnp.float32) ** level_of(key_of[8], (NODES,), ((0, 128),), -0.2, 0.2)), 0.2, 1.0)
    rate_left = bell_draw(key_of[9], (SPECIES, REACTIONS), SPECIES ** -0.5, 1.0, jnp.float32)
    rate_right = bell_draw(key_of[10], (SPECIES, REACTIONS), SPECIES ** -0.5, 1.0, jnp.float32)
    stoich = bell_draw(key_of[11], (REACTIONS, SPECIES), REACTIONS ** -0.5, 0.75, jnp.float32)
    return dict(state=state, lat_coef=lat_coef, diffusion=diffusion, layer_count=layer_count, species_scale=species_scale, stream=stream, reach_owner=reach_owner, reach_local=reach_local, exch_coef=exch_coef, rate_left=rate_left, rate_right=rate_right, stoich=stoich)


def column_slab(inputs, species_scale, rate_left, rate_right, stoich):
    rhs_slab, diff_slab, count_slab = inputs
    ncol = rhs_slab.shape[0]
    rhs3 = rhs_slab.reshape(ncol, LAYERS, SPECIES).transpose(0, 2, 1)
    level = jnp.arange(LAYERS, dtype=jnp.int32)
    active = (level[None, :] + 1 < count_slab[:, None]).astype(jnp.float32)
    iface = diff_slab * active
    upper = iface[:, None, :] * species_scale[None, :, None]
    lower = jnp.concatenate([jnp.zeros((ncol, SPECIES, 1), jnp.float32), upper[:, :, :-1]], axis=2)
    solved = lax.linalg.tridiagonal_solve(-lower, 1.0 + upper + lower, -upper, rhs3[..., None])[..., 0]
    conc = solved.transpose(0, 2, 1).reshape(ncol * LAYERS, SPECIES)
    hp = lax.Precision.HIGHEST
    rates = jnp.dot(conc, rate_left, precision=hp) * jnp.dot(conc, rate_right, precision=hp)
    change = jnp.dot(rates, stoich, precision=hp)
    cellmask = (level[None, :] < count_slab[:, None]).astype(jnp.float32).reshape(ncol * LAYERS, 1)
    return (conc + 0.1 * cellmask * change).reshape(ncol, LAYERS * SPECIES)

def reference(state, lat_coef, diffusion, layer_count, species_scale, stream, reach_owner, reach_local, exch_coef, rate_left, rate_right, stoich):
    owner = reach_owner[:, 0]
    ix = owner // N_GY * CX + reach_local // CY
    iy = owner % N_GY * CY + reach_local % CY
    top = state[:, :, :SPECIES]
    flux = exch_coef[:, None] * (stream - top[ix, iy])
    stream_out = stream - 0.5 * flux
    source = jnp.zeros((NX, NY, SPECIES), jnp.float32).at[ix, iy].add(flux)
    padded = jnp.pad(state, ((1, 1), (1, 1), (0, 0)))
    beside = padded[2:, 1:-1] + padded[:-2, 1:-1] + padded[1:-1, 2:] + padded[1:-1, :-2]
    rhs = state + lat_coef[:, :, None] * (beside - 4.0 * state)
    rhs = rhs.at[:, :, :SPECIES].add(source)
    state_out = lax.map(lambda inputs: column_slab(inputs, species_scale, rate_left, rate_right, stoich), (rhs, diffusion, layer_count))
    return (state_out, stream_out)
```

```python
import functools

import jax
import jax.numpy as jnp
from jax import lax
from jax.experimental import pallas as pl
from jax.experimental.pallas import tpu as pltpu
from jax.sharding import PartitionSpec as P

MESH = pl.DeviceIdType.MESH
f32, bf16, i32 = jnp.float32, jnp.bfloat16, jnp.int32
VM = pl.BlockSpec(memory_space=pltpu.VMEM)
ANY = pl.BlockSpec(memory_space=pl.ANY)

CAP = 64
ROWS = 16
MSG = ROWS + 1


def iota(shape, dim):
    return lax.broadcasted_iota(i32, shape, dim)


def split(x):
    hi = x.astype(bf16)
    return hi, (x - hi.astype(f32)).astype(bf16)


def dot(a, b):
    return jnp.dot(a, b, preferred_element_type=f32)


def pack_kernel(owner, local, coef, stream_t, flat_out, msg, rows, buf, flat_v, flat_s, sem):
    groups = owner.shape[0]
    peers = msg.shape[0]
    sub, lane = iota((128, 128), 0), iota((128, 128), 1)
    upto = (sub <= lane).astype(bf16)
    ones = jnp.ones((128, 128), bf16)
    carry = jnp.zeros((128, 128), f32)
    for g in range(groups):
        mine = sub == owner[g : g + 1, :]
        onehot = mine.astype(f32).astype(bf16)
        count = dot(onehot, upto) + carry
        carry = carry + dot(onehot, ones)
        rank = jnp.sum(jnp.where(mine, count, 0.0), axis=0, keepdims=True)
        flat_v[g : g + 1, :] = owner[g : g + 1, :] * CAP + rank.astype(i32) - 1
    pltpu.make_async_copy(flat_v, flat_s, sem).start()
    flat_out[...] = flat_v[...]

    def fill(g, _):
        at = pl.multiple_of(g * 128, 128)
        block = jnp.concatenate(
            [
                stream_t[:, pl.ds(at, 128)],
                local[pl.ds(g, 1), :].astype(f32),
                coef[pl.ds(g, 1), :],
                jnp.zeros((94, 128), f32),
            ],
            axis=0,
        )
        rows[pl.ds(at, 128), :] = block.T
        return 0

    lax.fori_loop(0, groups, fill, 0)
    empty = jnp.where(lane == 32, -1.0, 0.0)

    def clear(g, _):
        buf[pl.ds(pl.multiple_of(g * 128, 128), 128), :] = empty
        return 0

    lax.fori_loop(0, buf.shape[0] // 128, clear, 0)
    pltpu.make_async_copy(flat_v, flat_s, sem).wait()

    def move(g, _):
        for j in range(128):
            buf[pl.ds(flat_s[g, j], 1), :] = rows[pl.ds(g * 128 + j, 1), :]
        return 0

    lax.fori_loop(0, groups, move, 0)
    lane16 = iota((16, 128), 1)
    mine16 = lane16 // 8 == (16 - iota((16, 128), 0)) % 16

    def form(t, _):
        at = pl.multiple_of(t * CAP, CAP)
        part = [buf[pl.ds(at + q * 16, 16), :] for q in range(4)]
        vals = part[3]
        vals = pltpu.roll(vals, 96, axis=1)
        for q in (2, 1):
            vals = jnp.where(lane16 < 32 * (q + 1), pltpu.roll(part[q], 32 * q, axis=1), vals)
        vals = jnp.where(lane16 < 32, part[0], vals)
        meta = jnp.zeros((16, 128), f32)
        for q in range(4):
            moved = pltpu.roll(part[q], (96 + 2 * q) % 128, axis=1)
            meta = jnp.where((lane16 >= 2 * q) & (lane16 < 2 * q + 2), moved, meta)
        for shift in (8, 16, 32, 64):
            meta = meta + pltpu.roll(meta, shift, axis=1)
        meta = jnp.where(mine16, meta, 0.0)
        msg[pl.ds(t, 1), pl.ds(0, ROWS), :] = vals[None]
        msg[pl.ds(t, 1), pl.ds(ROWS, 1), :] = jnp.sum(meta, axis=0, keepdims=True)[None]
        return 0

    lax.fori_loop(0, peers, form, 0, unroll=4)


def pack(owner, local, coef, stream_t, peers):
    groups = owner.shape[0]
    return pl.pallas_call(
        pack_kernel,
        out_shape=(
            jax.ShapeDtypeStruct((groups, 128), i32),
            jax.ShapeDtypeStruct((peers, MSG, 128), f32),
        ),
        in_specs=[VM] * 4,
        out_specs=(VM, VM),
        scratch_shapes=[
            pltpu.VMEM((groups * 128, 128), f32),
            pltpu.VMEM((peers * CAP, 128), f32),
            pltpu.VMEM((groups, 128), i32),
            pltpu.SMEM((groups, 128), i32),
            pltpu.SemaphoreType.DMA,
        ],
        compiler_params=pltpu.CompilerParams(vmem_limit_bytes=48 << 20),
        name="pack",
    )(owner, local, coef, stream_t)


GROUP = 4


def flux_of(messages, top, acc, put):
    columns = top.shape[0]
    lane16 = iota((16, 128), 1)
    vals, cols, coefs = [], [], []
    for m in messages:
        meta = jnp.broadcast_to(m[ROWS : ROWS + 1, :], (16, 128))
        meta = pltpu.roll(meta, 0, axis=1, stride=8, stride_axis=0)
        for q in range(4):
            vals.append(pltpu.roll(m[0:ROWS, :], (128 - 32 * q) % 128, axis=1) if q else m[0:ROWS, :])
            cols.append(jnp.broadcast_to(meta[:, 2 * q : 2 * q + 1], (16, 128)))
            coefs.append(jnp.broadcast_to(meta[:, 2 * q + 1 : 2 * q + 2], (16, 128)))
    vals = jnp.concatenate(vals, axis=0)
    cols = jnp.concatenate(cols, axis=0)
    coefs = jnp.concatenate(coefs, axis=0)
    slots = vals.shape[0]
    lane = iota((slots, 128), 1).astype(f32)
    onehot = jnp.concatenate(
        [jnp.where(cols == lane + 128.0 * b, 1.0, 0.0).astype(bf16) for b in range(columns // 128)], axis=1
    )
    picked = dot(onehot, top[...])
    picked = picked + pltpu.roll(picked, 96, axis=1)
    flux = jnp.where(lane < 32.0, coefs * (vals - picked), 0.0)
    low = flux - flux.astype(bf16).astype(f32)
    both = flux.astype(bf16).astype(f32) + pltpu.roll(low, 32, axis=1)
    both = both.T[0:64, :].astype(bf16)
    acc[...] += dot(both, onehot)
    for p in range(len(messages)):
        out = flux[64 * p : 64 * p + 16, :]
        for q in range(1, 4):
            out = out + pltpu.roll(flux[64 * p + 16 * q : 64 * p + 16 * q + 16, :], 32 * q, axis=1)
        put(p, out)


def top_of(state_top, top):
    high, low = split(state_top)
    lane = iota(state_top.shape, 1)
    high, low = high.astype(f32), pltpu.roll(low.astype(f32), 32, axis=1)
    top[...] = jnp.where(lane < 32, high, jnp.where(lane < 64, low, 0.0)).astype(bf16)


def exchange_kernel(
    msg, state_top, source, back, inbox, outbox, top, acc, send1, recv1, send2, recv2
):
    peers = msg.shape[0]
    size_y = lax.axis_size("gy")
    me = lax.axis_index("gx") * size_y + lax.axis_index("gy")

    def device(t):
        return (t // size_y, lax.rem(t, size_y))

    def send(d):
        to = lax.rem(me + d, peers)
        return pltpu.make_async_remote_copy(
            src_ref=msg.at[to],
            dst_ref=inbox.at[d],
            send_sem=send1,
            recv_sem=recv1.at[d],
            device_id=device(to),
            device_id_type=MESH,
        )

    def reply(d):
        to = lax.rem(me + peers - d, peers)
        return pltpu.make_async_remote_copy(
            src_ref=outbox.at[d],
            dst_ref=back.at[me],
            send_sem=send2,
            recv_sem=recv2,
            device_id=device(to),
            device_id_type=MESH,
        )

    def start(d, _):
        send(d).start()
        return 0

    lax.fori_loop(1, peers, start, 0)
    keep = pltpu.make_async_copy(msg.at[me], inbox.at[0], recv1.at[0])
    keep.start()
    columns = state_top.shape[0] * state_top.shape[1]
    top_of(state_top[...].reshape(columns, 128), top)
    acc[...] = jnp.zeros_like(acc)
    keep.wait()

    def work(c, first):
        for p in range(GROUP):
            if not (first and p == 0):
                send(c * GROUP + p).wait_recv()

        def put(p, value):
            outbox[pl.ds(c * GROUP + p, 1)] = value[None]

        flux_of([inbox[c * GROUP + p] for p in range(GROUP)], top, acc, put)
        for p in range(GROUP):
            if not (first and p == 0):
                reply(c * GROUP + p).start()

    work(0, True)

    def step(c, _):
        work(c, False)
        return 0

    lax.fori_loop(1, peers // GROUP, step, 0)
    own = pltpu.make_async_copy(outbox.at[0], back.at[me], recv1.at[0])
    own.start()
    source[...] = acc[0:32, :] + acc[32:64, :]
    own.wait()
    rest = pl.ds(0, peers - 1)
    pltpu.make_async_copy(msg.at[rest], msg.at[rest], send1).wait()
    pltpu.make_async_copy(outbox.at[rest], outbox.at[rest], send2).wait()
    pltpu.make_async_copy(back.at[rest], back.at[rest], recv2).wait()


def exchange(msg, state):
    peers = msg.shape[0]
    tile_x, tile_y, _ = state.shape
    columns = tile_x * tile_y
    return pl.pallas_call(
        exchange_kernel,
        grid=(1,),
        out_shape=(
            jax.ShapeDtypeStruct((32, columns), f32),
            jax.ShapeDtypeStruct((peers, ROWS, 128), f32),
        ),
        in_specs=[VM, pl.BlockSpec((tile_x, tile_y, 128), lambda i: (0, 0, 0))],
        out_specs=(VM, VM),
        scratch_shapes=[
            pltpu.VMEM((peers, MSG, 128), f32),
            pltpu.VMEM((peers, ROWS, 128), f32),
            pltpu.VMEM((columns, 128), bf16),
            pltpu.VMEM((64, columns), f32),
            pltpu.SemaphoreType.DMA,
            pltpu.SemaphoreType.DMA((peers,)),
            pltpu.SemaphoreType.DMA,
            pltpu.SemaphoreType.DMA,
        ],
        compiler_params=pltpu.CompilerParams(has_side_effects=True, vmem_limit_bytes=48 << 20),
        name="exchange",
    )(msg, state)


def unpack_kernel(flat, back, stream_t, out, buf, rows):
    groups = flat.shape[0]
    peers = back.shape[0]

    def spread(t, _):
        m = back[t]
        at = pl.multiple_of(t * CAP, CAP)
        for q in range(4):
            buf[pl.ds(at + 16 * q, 16), :] = pltpu.roll(m, 128 - 32 * q, axis=1) if q else m
        return 0

    lax.fori_loop(0, peers, spread, 0, unroll=4)

    def move(g, _):
        at = pl.multiple_of(g * 128, 128)
        for j in range(128):
            rows[pl.ds(j, 1), :] = buf[pl.ds(flat[g, j], 1), :]
        out[:, pl.ds(at, 128)] = stream_t[:, pl.ds(at, 128)] - 0.5 * rows[...].T[0:32, :]
        return 0

    lax.fori_loop(0, groups, move, 0)


def unpack(flat, back, stream_t):
    peers = back.shape[0]
    return pl.pallas_call(
        unpack_kernel,
        out_shape=jax.ShapeDtypeStruct(stream_t.shape, f32),
        in_specs=[pl.BlockSpec(memory_space=pltpu.SMEM), VM, VM],
        out_specs=VM,
        scratch_shapes=[pltpu.VMEM((peers * CAP, 128), f32), pltpu.VMEM((128, 128), f32)],
        compiler_params=pltpu.CompilerParams(vmem_limit_bytes=48 << 20),
        name="unpack",
    )(flat, back, stream_t)


XB = 8


def columns_kernel(
    st, up, dn, x_low, x_high, y_low, y_high, lat, count, diff, scale, source, left, right, stoich_t,
    out, w_first, w_low, s_high, s_low, lat_col, count_col, scale_col, rhs, coef, iface,
):
    i = pl.program_id(0)
    last = pl.num_programs(0) - 1
    sub, lane = iota((128, 128), 0), iota((128, 128), 1)

    @pl.when(i == 0)
    def _():
        inside = iota((128, 256), 0) // 32 == iota((128, 256), 1) // 64

        def spread(w):
            wide = jnp.concatenate([w] * 4, axis=1)
            return jnp.where(inside, jnp.concatenate([wide] * 4, axis=0), 0.0)

        high, low = split(jnp.concatenate([spread(left[...]), spread(right[...])], axis=1))
        w_first[0:128, :] = high
        w_first[128:256, :] = high
        w_low[...] = low
        high, low = split(spread(stoich_t[...]).T)
        s_high[...] = high
        s_low[...] = low

        def turned(a):
            a = jnp.concatenate([a, jnp.zeros((32, 96), f32)], axis=1)
            return jnp.concatenate([a, jnp.zeros((96, 128), f32)], axis=0).T

        lat_t, count_t = turned(lat[...]), turned(count[...].astype(f32))
        for g in range(4):
            lat_col[g] = pltpu.roll(lat_t, (128 - XB * g) % 128, axis=1)[0:32, :]
            count_col[g] = pltpu.roll(count_t, (128 - XB * g) % 128, axis=1)[0:32, :]
        scale_col[...] = jnp.broadcast_to(
            jnp.sum(
                jnp.where(iota((32, 32), 0) == iota((32, 32), 1), jnp.broadcast_to(scale[...], (32, 32)), 0.0),
                axis=1,
                keepdims=True,
            ),
            (32, 128),
        )

    row = iota((32, 128), 0)
    lats = [jnp.broadcast_to(lat_col[i, :, x : x + 1], (32, 128)) for x in range(XB)]
    for cb in range(2):
        for j in range(16):
            at = slice(128 * j, 128 * j + 128)
            parts = []
            for x in range(4 * cb, 4 * cb + 4):
                s = st[x, :, at]
                before = st[x - 1, :, at] if x else jnp.where(i == 0, x_low[0, :, at], up[0, :, at])
                after = st[x + 1, :, at] if x < XB - 1 else jnp.where(i == last, x_high[0, :, at], dn[0, :, at])
                lower = jnp.where(row == 0, y_low[x, :, at], pltpu.roll(s, 1, axis=0))
                upper = jnp.where(row == 31, y_high[x, :, at], pltpu.roll(s, 31, axis=0))
                parts.append(s + lats[x] * ((before + after) + (lower + upper) - 4.0 * s))
            rhs[at, 128 * cb : 128 * cb + 128] = jnp.concatenate(parts, axis=0).T
        counts = jnp.concatenate([count[pl.ds(XB * i + 4 * cb + x, 1), :] for x in range(4)], axis=1)
        d = diff[4 * cb : 4 * cb + 4].reshape(128, 64)
        d = jnp.concatenate([d, jnp.zeros((128, 64), f32)], axis=1).T[0:64, :]
        iface[:, 128 * cb : 128 * cb + 128] = jnp.where(iota((64, 128), 0) + 1 < counts, d, 0.0)
    rhs[0:32, :] += source[...]

    scales = jnp.concatenate([scale_col[...]] * 2, axis=1)
    zero = jnp.zeros((32, 256), f32)

    def upper_at(k):
        return scales * iface[k : k + 1, :]

    def cell(k):
        return slice(32 * k, 32 * k + 32)

    c, d, u_before = zero, zero, zero
    e_c, e_d, u_here = zero, zero, upper_at(63)
    for k in range(32):
        u = upper_at(k)
        r = 1.0 / (1.0 + u + u_before * (1.0 - c))
        d = (rhs[cell(k), :] + u_before * d) * r
        c = u * r
        u_before = u
        m = 63 - k
        v = upper_at(m - 1)
        r = 1.0 / (1.0 + v + u_here * (1.0 - e_c))
        e_d = (rhs[cell(m), :] + u_here * e_d) * r
        e_c = v * r
        u_here = v
        if k < 31:
            coef[cell(k), :] = c
            rhs[cell(k), :] = d
            coef[cell(m), :] = e_c
            rhs[cell(m), :] = e_d
    low = (d + c * e_d) / (1.0 - c * e_c)
    high = e_d + e_c * low
    rhs[cell(31), :] = low
    rhs[cell(32), :] = high
    for k in range(30, -1, -1):
        low = rhs[cell(k), :] + coef[cell(k), :] * low
        rhs[cell(k), :] = low
        m = 63 - k
        high = rhs[cell(m), :] + coef[cell(m), :] * high
        rhs[cell(m), :] = high

    for cb in range(2):
        counts = jnp.concatenate(
            [jnp.broadcast_to(count_col[i, :, x : x + 1], (32, 128)) for x in range(4 * cb, 4 * cb + 4)], axis=0
        )
        depth = counts - (lane // 32).astype(f32)
        for j in range(16):
            at = slice(128 * j, 128 * j + 128)
            x = rhs[at, 128 * cb : 128 * cb + 128].T
            high, low = split(x)
            both = dot(jnp.concatenate([high, low], axis=1), w_first[...]) + dot(high, w_low[...])
            high, low = split(both[:, 0:256] * both[:, 256:512])
            change = dot(high, s_high[...]) + dot(low, s_high[...]) + dot(high, s_low[...])
            new = x + jnp.where(depth > 4.0 * j, 0.1, 0.0) * change
            for p in range(4):
                out[4 * cb + p, :, at] = new[32 * p : 32 * p + 32, :]


def columns(state, x_low, x_high, y_low, y_high, lat, count, diffusion, scale, source, left, right, stoich_t):
    tile_x, tile_y, width = state.shape
    steps = tile_x // XB
    whole = lambda shape: pl.BlockSpec(shape, lambda i: (0,) * len(shape))
    return pl.pallas_call(
        columns_kernel,
        grid=(steps,),
        out_shape=jax.ShapeDtypeStruct(state.shape, f32),
        in_specs=[
            pl.BlockSpec((XB, tile_y, width), lambda i: (i, 0, 0)),
            pl.BlockSpec((1, tile_y, width), lambda i: (jnp.maximum(XB * i - 1, 0), 0, 0)),
            pl.BlockSpec((1, tile_y, width), lambda i: (jnp.minimum(XB * i + XB, tile_x - 1), 0, 0)),
            whole(x_low.shape),
            whole(x_high.shape),
            pl.BlockSpec((XB, 1, width), lambda i: (i, 0, 0)),
            pl.BlockSpec((XB, 1, width), lambda i: (i, 0, 0)),
            whole(lat.shape),
            whole(count.shape),
            pl.BlockSpec((XB, tile_y, diffusion.shape[2]), lambda i: (i, 0, 0)),
            whole(scale.shape),
            pl.BlockSpec((32, XB * tile_y), lambda i: (0, i)),
            whole(left.shape),
            whole(right.shape),
            whole(stoich_t.shape),
        ],
        out_specs=pl.BlockSpec((XB, tile_y, width), lambda i: (i, 0, 0)),
        scratch_shapes=[
            pltpu.VMEM((256, 512), bf16),
            pltpu.VMEM((128, 512), bf16),
            pltpu.VMEM((256, 128), bf16),
            pltpu.VMEM((256, 128), bf16),
            pltpu.VMEM((steps, 32, 128), f32),
            pltpu.VMEM((steps, 32, 128), f32),
            pltpu.VMEM((32, 128), f32),
            pltpu.VMEM((width, XB * tile_y), f32),
            pltpu.VMEM((width, XB * tile_y), f32),
            pltpu.VMEM((64, XB * tile_y), f32),
        ],
        compiler_params=pltpu.CompilerParams(vmem_limit_bytes=56 << 20),
        name="columns",
    )(state, state, state, x_low, x_high, y_low, y_high, lat, count, diffusion, scale, source, left, right, stoich_t)


def halo(state):
    out = []
    for axis, dim in (("gx", 0), ("gy", 1)):
        count = lax.axis_size(axis)
        forward = [(i, i + 1) for i in range(count - 1)]
        backward = [(target, source) for source, target in forward]
        end = state.shape[dim] - 1
        out.append(lax.ppermute(lax.slice_in_dim(state, end, end + 1, axis=dim), axis, forward))
        out.append(lax.ppermute(lax.slice_in_dim(state, 0, 1, axis=dim), axis, backward))
    return out


def body(
    state,
    lat_coef,
    diffusion,
    layer_count,
    species_scale,
    stream,
    reach_owner,
    reach_local,
    exch_coef,
    rate_left,
    rate_right,
    stoich,
):
    peers = lax.axis_size("gx") * lax.axis_size("gy")
    x_low, x_high, y_low, y_high = halo(state)
    stream_t = stream.T
    flat, msg = pack(
        reach_owner.reshape(-1, 128), reach_local.reshape(-1, 128), exch_coef.reshape(-1, 128), stream_t, peers
    )
    source, back = exchange(msg, state)
    state_out = columns(
        state, x_low, x_high, y_low, y_high, lat_coef, layer_count, diffusion, species_scale[None, :], source,
        rate_left, rate_right, stoich.T,
    )
    stream_out = unpack(flat, back, stream_t).T
    return (state_out, stream_out)


def solution(mesh):
    return jax.shard_map(
        body,
        mesh=mesh,
        in_specs=(
            P("gx", "gy", None),
            P("gx", "gy"),
            P("gx", "gy", None),
            P("gx", "gy"),
            P(),
            P(("gx", "gy"), None),
            P(("gx", "gy"), None),
            P(("gx", "gy")),
            P(("gx", "gy")),
            P(),
            P(),
            P(),
        ),
        out_specs=(P("gx", "gy", None), P(("gx", "gy"), None)),
        check_vma=False,
    )
```

```python
import functools

import jax
import jax.numpy as jnp
from jax import lax
from jax.experimental import pallas as pl
from jax.experimental.pallas import tpu as pltpu
from jax.sharding import PartitionSpec as P

MESH = pl.DeviceIdType.MESH
f32, bf16, i32 = jnp.float32, jnp.bfloat16, jnp.int32
VM = pl.BlockSpec(memory_space=pltpu.VMEM)
ANY = pl.BlockSpec(memory_space=pl.ANY)

CAP = 64
ROWS = 16
MSG = ROWS + 1
FORM = 16
BATCH = 8


def iota(shape, dim):
    return lax.broadcasted_iota(i32, shape, dim)


def split(x):
    hi = x.astype(bf16)
    return hi, (x - hi.astype(f32)).astype(bf16)


def dot(a, b):
    return jnp.dot(a, b, preferred_element_type=f32)


def pack_kernel(owner, local, coef, stream_t, flat_out, msg, rows, buf, flat_v, flat_s, sem):
    groups = owner.shape[0]
    peers = msg.shape[0]
    sub, lane = iota((128, 128), 0), iota((128, 128), 1)
    upto = (sub <= lane).astype(bf16)
    ones = jnp.ones((128, 128), bf16)
    carry = jnp.zeros((128, 128), f32)
    for g in range(groups):
        mine = sub == owner[g : g + 1, :]
        onehot = mine.astype(f32).astype(bf16)
        count = dot(onehot, upto) + carry
        carry = carry + dot(onehot, ones)
        rank = jnp.sum(jnp.where(mine, count, 0.0), axis=0, keepdims=True)
        flat_v[g : g + 1, :] = owner[g : g + 1, :] * CAP + rank.astype(i32) - 1
    pltpu.make_async_copy(flat_v, flat_s, sem).start()
    flat_out[...] = flat_v[...]

    def fill(g, _):
        at = pl.multiple_of(g * 128, 128)
        block = jnp.concatenate(
            [
                stream_t[:, pl.ds(at, 128)],
                local[pl.ds(g, 1), :].astype(f32),
                coef[pl.ds(g, 1), :],
                jnp.zeros((94, 128), f32),
            ],
            axis=0,
        )
        rows[pl.ds(at, 128), :] = block.T
        return 0

    lax.fori_loop(0, groups, fill, 0)
    empty = jnp.where(lane == 32, -1.0, 0.0)

    def clear(g, _):
        buf[pl.ds(pl.multiple_of(g * 128, 128), 128), :] = empty
        return 0

    lax.fori_loop(0, buf.shape[0] // 128, clear, 0)
    pltpu.make_async_copy(flat_v, flat_s, sem).wait()

    def move(g, _):
        for j in range(128):
            buf[pl.ds(flat_s[g, j], 1), :] = rows[pl.ds(g * 128 + j, 1), :]
        return 0

    lax.fori_loop(0, groups, move, 0)
    lanes = iota((FORM * 16, 128), 1)
    spot = lanes // 8 == (16 - iota((FORM * 16, 128), 0) % 16) % 16

    def form(t, _):
        at = pl.multiple_of(t * FORM * CAP, FORM * CAP)
        part = buf[pl.ds(at, FORM * CAP), :].reshape(FORM, 4, 16, 128)
        part = [part[:, q].reshape(FORM * 16, 128) for q in range(4)]
        vals = pltpu.roll(part[3], 96, axis=1)
        for q in (2, 1):
            vals = jnp.where(lanes < 32 * (q + 1), pltpu.roll(part[q], 32 * q, axis=1), vals)
        vals = jnp.where(lanes < 32, part[0], vals)
        meta = jnp.zeros((FORM * 16, 128), f32)
        for q in range(4):
            moved = pltpu.roll(part[q], (96 + 2 * q) % 128, axis=1)
            meta = jnp.where((lanes >= 2 * q) & (lanes < 2 * q + 2), moved, meta)
        for shift in (8, 16, 32, 64):
            meta = meta + pltpu.roll(meta, shift, axis=1)
        meta = jnp.sum(jnp.where(spot, meta, 0.0).reshape(FORM, 16, 128), axis=1)
        to = pl.ds(pl.multiple_of(t * FORM, FORM), FORM)
        msg[to, pl.ds(0, ROWS), :] = vals.reshape(FORM, 16, 128)
        msg[to, pl.ds(ROWS, 1), :] = meta[:, None, :]
        return 0

    lax.fori_loop(0, peers // FORM, form, 0)


def pack(owner, local, coef, stream_t, peers):
    groups = owner.shape[0]
    return pl.pallas_call(
        pack_kernel,
        out_shape=(
            jax.ShapeDtypeStruct((groups, 128), i32),
            jax.ShapeDtypeStruct((peers, MSG, 128), f32),
        ),
        in_specs=[VM] * 4,
        out_specs=(VM, VM),
        scratch_shapes=[
            pltpu.VMEM((groups * 128, 128), f32),
            pltpu.VMEM((peers * CAP, 128), f32),
            pltpu.VMEM((groups, 128), i32),
            pltpu.SMEM((groups, 128), i32),
            pltpu.SemaphoreType.DMA,
        ],
        compiler_params=pltpu.CompilerParams(vmem_limit_bytes=48 << 20),
        name="pack",
    )(owner, local, coef, stream_t)


def flux_of(messages, top, acc, put):
    count = len(messages)
    rows = count * ROWS
    lane = iota((rows, 128), 1)
    lane_f, place, side = lane.astype(f32), lane // 32, (lane // 64).astype(f32)
    vals = jnp.concatenate([m[0:ROWS, :] for m in messages], axis=0)
    meta = jnp.concatenate(
        [
            pltpu.roll(jnp.broadcast_to(m[ROWS : ROWS + 1, :], (ROWS, 128)), 0, axis=1, stride=8, stride_axis=0)
            for m in messages
        ],
        axis=0,
    )

    def by_place(parts):
        out = parts[3]
        for q in (2, 1, 0):
            out = jnp.where(place == q, parts[q], out)
        return out

    onehots, parts, coefs = [], [], []
    for q in range(4):
        column = jnp.broadcast_to(meta[:, 2 * q : 2 * q + 1], (rows, 128))
        part = jnp.floor(column * (1.0 / 256.0))
        low = column - 256.0 * part
        onehots.append(
            jnp.concatenate(
                [jnp.where(low == lane_f + 128.0 * b, 1.0, 0.0).astype(bf16) for b in range(2)], axis=1
            )
        )
        parts.append(part)
        coefs.append(jnp.broadcast_to(meta[:, 2 * q + 1 : 2 * q + 2], (rows, 128)))
    onehot = jnp.concatenate(onehots, axis=0)
    picked = dot(onehot, top[...])
    tops = []
    for q in range(4):
        p = picked[rows * q : rows * q + rows, :]
        p = jnp.where(parts[q] == side, p[:, 0:128], 0.0) + jnp.where(parts[q] == side + 2.0, p[:, 128:256], 0.0)
        p = p + pltpu.roll(p, 64, axis=1)
        tops.append(p + pltpu.roll(p, 32, axis=1))
    flux = by_place(coefs) * (vals - by_place(tops))
    for p in range(count):
        put(p, flux[ROWS * p : ROWS * p + ROWS, :])
    flux_t, part_t = flux.T, by_place(parts).T
    flux_t = jnp.concatenate([flux_t[32 * q : 32 * q + 32, :] for q in range(4)], axis=1)
    part_t = jnp.concatenate([part_t[32 * q : 32 * q + 1, :] for q in range(4)], axis=1)
    high = flux_t.astype(bf16).astype(f32)
    both = jnp.concatenate([high, flux_t - high], axis=0)
    spread = jnp.concatenate([jnp.where(part_t == float(g), both, 0.0).astype(bf16) for g in range(4)], axis=0)
    acc[...] += dot(spread, onehot)


def top_of(state_top, top):
    lane = iota((256, 128), 1)
    quarters = []
    for g in range(4):
        t = jnp.where(lane < 32, state_top[256 * g : 256 * g + 256, :], 0.0)
        high = t.astype(bf16).astype(f32)
        quarters.append(high + pltpu.roll(t - high, 32, axis=1))
    top[...] = jnp.concatenate(
        [quarters[g] + pltpu.roll(quarters[g + 1], 64, axis=1) for g in (0, 2)], axis=1
    ).astype(bf16)


def source_of(acc, source):
    for g in range(4):
        source[:, 256 * g : 256 * g + 256] = acc[64 * g : 64 * g + 32, :] + acc[64 * g + 32 : 64 * g + 64, :]


def exchange_kernel(
    msg, state_top, state, none_x, none_y, source, back, x_low, x_high, y_low, y_high,
    inbox, outbox, top, acc, send1, recv1, send2, recv2, send_edge, recv_edge,
):
    peers = msg.shape[0]
    size_x = lax.axis_size("gx")
    ends = state.shape[0] - 1, state.shape[1] - 1
    size_y = lax.axis_size("gy")
    me = lax.axis_index("gx") * size_y + lax.axis_index("gy")

    def device(t):
        return (t // size_y, lax.rem(t, size_y))

    def send(d):
        to = lax.rem(me + d, peers)
        return pltpu.make_async_remote_copy(
            src_ref=msg.at[to],
            dst_ref=inbox.at[d],
            send_sem=send1,
            recv_sem=recv1.at[d],
            device_id=device(to),
            device_id_type=MESH,
        )

    def reply(d):
        to = lax.rem(me + peers - d, peers)
        return pltpu.make_async_remote_copy(
            src_ref=outbox.at[d],
            dst_ref=back.at[me],
            send_sem=send2,
            recv_sem=recv2,
            device_id=device(to),
            device_id_type=MESH,
        )

    gx, gy = lax.axis_index("gx"), lax.axis_index("gy")
    edges = [
        (state.at[pl.ds(ends[0], 1)], x_low, (lax.rem(gx + 1, size_x), gy), gx < size_x - 1, gx > 0),
        (state.at[pl.ds(0, 1)], x_high, (lax.rem(gx + size_x - 1, size_x), gy), gx > 0, gx < size_x - 1),
        (state.at[:, pl.ds(ends[1], 1)], y_low, (gx, lax.rem(gy + 1, size_y)), gy < size_y - 1, gy > 0),
        (state.at[:, pl.ds(0, 1)], y_high, (gx, lax.rem(gy + size_y - 1, size_y)), gy > 0, gy < size_y - 1),
    ]

    def edge(n):
        block, to, device_id, _, _ = edges[n]
        return pltpu.make_async_remote_copy(
            src_ref=block,
            dst_ref=to,
            send_sem=send_edge.at[n],
            recv_sem=recv_edge.at[n],
            device_id=device_id,
            device_id_type=MESH,
        )

    def outside(n):
        return pltpu.make_async_copy(none_x if n < 2 else none_y, edges[n][1], recv_edge.at[n])

    def start(d, _):
        send(d).start()
        return 0

    lax.fori_loop(1, peers, start, 0)
    for n in range(4):
        pl.when(edges[n][3])(edge(n).start)
        pl.when(jnp.logical_not(edges[n][4]))(outside(n).start)
    keep = pltpu.make_async_copy(msg.at[me], inbox.at[0], recv1.at[0])
    keep.start()
    columns = state_top.shape[0] * state_top.shape[1]
    top_of(state_top[...].reshape(columns, 128), top)
    acc[...] = jnp.zeros_like(acc)
    keep.wait()

    def work(c, first):
        for p in range(BATCH):
            if not (first and p == 0):
                send(c * BATCH + p).wait_recv()

        def put(p, value):
            outbox[pl.ds(c * BATCH + p, 1)] = value[None]

        flux_of([inbox[c * BATCH + p] for p in range(BATCH)], top, acc, put)
        for p in range(BATCH):
            if not (first and p == 0):
                reply(c * BATCH + p).start()

    work(0, True)

    def step(c, _):
        work(c, False)
        return 0

    lax.fori_loop(1, peers // BATCH, step, 0)
    own = pltpu.make_async_copy(outbox.at[0], back.at[me], recv1.at[0])
    own.start()
    source_of(acc, source)
    own.wait()
    for n in range(4):
        pl.when(edges[n][3])(edge(n).wait_send)
        pl.when(edges[n][4])(edge(n).wait_recv)
        pl.when(jnp.logical_not(edges[n][4]))(outside(n).wait)
    rest = pl.ds(0, peers - 1)
    pltpu.make_async_copy(msg.at[rest], msg.at[rest], send1).wait()
    pltpu.make_async_copy(outbox.at[rest], outbox.at[rest], send2).wait()
    pltpu.make_async_copy(back.at[rest], back.at[rest], recv2).wait()


def exchange(msg, state):
    peers = msg.shape[0]
    tile_x, tile_y, width = state.shape
    edge_x = jax.ShapeDtypeStruct((1, tile_y, width), f32)
    edge_y = jax.ShapeDtypeStruct((tile_x, 1, width), f32)
    return pl.pallas_call(
        exchange_kernel,
        grid=(1,),
        out_shape=(
            jax.ShapeDtypeStruct((32, tile_x * tile_y), f32),
            jax.ShapeDtypeStruct((peers, ROWS, 128), f32),
            edge_x,
            edge_x,
            edge_y,
            edge_y,
        ),
        in_specs=[VM, pl.BlockSpec((tile_x, tile_y, 128), lambda i: (0, 0, 0)), ANY, ANY, ANY],
        out_specs=(VM, VM, ANY, ANY, ANY, ANY),
        scratch_shapes=[
            pltpu.VMEM((peers, MSG, 128), f32),
            pltpu.VMEM((peers, ROWS, 128), f32),
            pltpu.VMEM((256, 256), bf16),
            pltpu.VMEM((256, 256), f32),
            pltpu.SemaphoreType.DMA,
            pltpu.SemaphoreType.DMA((peers,)),
            pltpu.SemaphoreType.DMA,
            pltpu.SemaphoreType.DMA,
            pltpu.SemaphoreType.DMA((4,)),
            pltpu.SemaphoreType.DMA((4,)),
        ],
        compiler_params=pltpu.CompilerParams(has_side_effects=True, vmem_limit_bytes=60 << 20),
        name="exchange",
    )(msg, state, state, jnp.zeros((1, tile_y, width), f32), jnp.zeros((tile_x, 1, width), f32))


def unpack_kernel(flat, back, stream_t, out, buf, rows):
    groups = flat.shape[0]
    peers = back.shape[0]

    def spread(t, _):
        m = back[t]
        at = pl.multiple_of(t * CAP, CAP)
        for q in range(4):
            buf[pl.ds(at + 16 * q, 16), :] = pltpu.roll(m, 128 - 32 * q, axis=1) if q else m
        return 0

    lax.fori_loop(0, peers, spread, 0, unroll=4)

    def move(g, _):
        at = pl.multiple_of(g * 128, 128)
        for j in range(128):
            rows[pl.ds(j, 1), :] = buf[pl.ds(flat[g, j], 1), :]
        out[:, pl.ds(at, 128)] = stream_t[:, pl.ds(at, 128)] - 0.5 * rows[...].T[0:32, :]
        return 0

    lax.fori_loop(0, groups, move, 0)


def unpack(flat, back, stream_t):
    peers = back.shape[0]
    return pl.pallas_call(
        unpack_kernel,
        out_shape=jax.ShapeDtypeStruct(stream_t.shape, f32),
        in_specs=[pl.BlockSpec(memory_space=pltpu.SMEM), VM, VM],
        out_specs=VM,
        scratch_shapes=[pltpu.VMEM((peers * CAP, 128), f32), pltpu.VMEM((128, 128), f32)],
        compiler_params=pltpu.CompilerParams(vmem_limit_bytes=48 << 20),
        name="unpack",
    )(flat, back, stream_t)


XB = 8
PART = 8


def columns_kernel(
    st, up, dn, x_low, x_high, y_low, y_high, lat, count, diff, scale, source, left, right, stoich_t,
    out, w_a, w_b, s_both, s_high, lat_col, count_col, scale_col, rhs, coef, iface,
):
    i = pl.program_id(0)
    last = pl.num_programs(0) - 1
    sub, lane = iota((128, 128), 0), iota((128, 128), 1)

    @pl.when(i == 0)
    def _():
        inside = iota((64, 128), 0) // 32 == iota((64, 128), 1) // 64

        def spread(w):
            return jnp.where(inside, jnp.concatenate([jnp.concatenate([w] * 2, axis=1)] * 2, axis=0), 0.0)

        pair = jnp.concatenate([spread(left[...]), spread(right[...])], axis=1)
        high, low = split(pair)
        none = jnp.zeros((64, 256), bf16)
        w_a[...] = jnp.concatenate([high, high, low, none], axis=0)
        w_b[...] = jnp.concatenate([high, high, none, low], axis=0)
        inside = iota((128, 256), 0) // 32 == iota((128, 256), 1) // 64
        wide = jnp.concatenate([stoich_t[...]] * 4, axis=1)
        high, low = split(jnp.where(inside, jnp.concatenate([wide] * 4, axis=0), 0.0).T)
        s_both[...] = jnp.concatenate([high, low], axis=1)
        s_high[...] = high

        def turned(a):
            a = jnp.concatenate([a, jnp.zeros((32, 96), f32)], axis=1)
            return jnp.concatenate([a, jnp.zeros((96, 128), f32)], axis=0).T

        lat_t, count_t = turned(lat[...]), turned(count[...].astype(f32))
        for g in range(4):
            lat_col[g] = pltpu.roll(lat_t, (128 - XB * g) % 128, axis=1)[0:32, :]
            count_col[g] = pltpu.roll(count_t, (128 - XB * g) % 128, axis=1)[0:32, :]
        scale_col[...] = jnp.broadcast_to(
            jnp.sum(
                jnp.where(iota((32, 32), 0) == iota((32, 32), 1), jnp.broadcast_to(scale[...], (32, 32)), 0.0),
                axis=1,
                keepdims=True,
            ),
            (32, 128),
        )

    row = iota((32, 128), 0)
    lats = [jnp.broadcast_to(lat_col[i, :, x : x + 1], (32, 128)) for x in range(XB)]
    for cb in range(2):
        for j in range(16):
            at = slice(128 * j, 128 * j + 128)
            parts = []
            for x in range(4 * cb, 4 * cb + 4):
                s = st[x, :, at]
                before = st[x - 1, :, at] if x else jnp.where(i == 0, x_low[0, :, at], up[0, :, at])
                after = st[x + 1, :, at] if x < XB - 1 else jnp.where(i == last, x_high[0, :, at], dn[0, :, at])
                lower = jnp.where(row == 0, y_low[x, :, at], pltpu.roll(s, 1, axis=0))
                upper = jnp.where(row == 31, y_high[x, :, at], pltpu.roll(s, 31, axis=0))
                parts.append(s + lats[x] * ((before + after) + (lower + upper) - 4.0 * s))
            rhs[at, 128 * cb : 128 * cb + 128] = jnp.concatenate(parts, axis=0).T
        counts = jnp.concatenate([count[pl.ds(XB * i + 4 * cb + x, 1), :] for x in range(4)], axis=1)
        d = diff[4 * cb : 4 * cb + 4].reshape(128, 64)
        d = jnp.concatenate([d, jnp.zeros((128, 64), f32)], axis=1).T[0:64, :]
        iface[:, 128 * cb : 128 * cb + 128] = jnp.where(iota((64, 128), 0) + 1 < counts, d, 0.0)
    rhs[0:32, :] += source[...]

    scales = jnp.concatenate([scale_col[...]] * 2, axis=1)
    zero = jnp.zeros((32, 256), f32)

    def upper_at(k):
        return scales * iface[k : k + 1, :]

    def cell(k):
        return slice(32 * k, 32 * k + 32)

    c, d, u_before = zero, zero, zero
    e_c, e_d, u_here = zero, zero, upper_at(63)
    for k in range(32):
        u = upper_at(k)
        r = 1.0 / (1.0 + u + u_before * (1.0 - c))
        d = (rhs[cell(k), :] + u_before * d) * r
        c = u * r
        u_before = u
        m = 63 - k
        v = upper_at(m - 1)
        r = 1.0 / (1.0 + v + u_here * (1.0 - e_c))
        e_d = (rhs[cell(m), :] + u_here * e_d) * r
        e_c = v * r
        u_here = v
        if k < 31:
            coef[cell(k), :] = c
            rhs[cell(k), :] = d
            coef[cell(m), :] = e_c
            rhs[cell(m), :] = e_d
    low = (d + c * e_d) / (1.0 - c * e_c)
    high = e_d + e_c * low
    rhs[cell(31), :] = low
    rhs[cell(32), :] = high
    for k in range(30, -1, -1):
        low = rhs[cell(k), :] + coef[cell(k), :] * low
        rhs[cell(k), :] = low
        m = 63 - k
        high = rhs[cell(m), :] + coef[cell(m), :] * high
        rhs[cell(m), :] = high

    half = lane < 64
    for cb in range(2):
        counts = jnp.concatenate(
            [jnp.broadcast_to(count_col[i, :, x : x + 1], (32, 128)) for x in range(4 * cb, 4 * cb + 4)], axis=0
        )
        depth = counts - (lane // 32).astype(f32)
        for first in range(0, 16, PART):
            solved, pair_a, pair_b = [], [], []
            for j in range(first, first + PART):
                x = rhs[128 * j : 128 * j + 128, 128 * cb : 128 * cb + 128].T
                high = x.astype(bf16)
                wide = high.astype(f32)
                low = pltpu.roll(x - wide, 64, axis=1)
                pair_a.append(jnp.concatenate([jnp.where(half, wide, low).astype(bf16), high], axis=1))
                pair_b.append(jnp.concatenate([jnp.where(half, low, wide).astype(bf16), high], axis=1))
                solved.append(x)
            both = dot(jnp.concatenate(pair_a, axis=0), w_a[...])
            rates_a = split(both[:, 0:128] * both[:, 128:256])
            both = dot(jnp.concatenate(pair_b, axis=0), w_b[...])
            rates_b = split(both[:, 0:128] * both[:, 128:256])
            change = dot(jnp.concatenate([rates_a[0], rates_b[0]], axis=1), s_both[...])
            change = change[:, 0:128] + change[:, 128:256]
            change = change + dot(jnp.concatenate([rates_a[1], rates_b[1]], axis=1), s_high[...])
            for n in range(PART):
                j = first + n
                new = solved[n] + jnp.where(depth > 4.0 * j, 0.1, 0.0) * change[128 * n : 128 * n + 128, :]
                for p in range(4):
                    out[4 * cb + p, :, 128 * j : 128 * j + 128] = new[32 * p : 32 * p + 32, :]


def columns(state, x_low, x_high, y_low, y_high, lat, count, diffusion, scale, source, left, right, stoich_t):
    tile_x, tile_y, width = state.shape
    steps = tile_x // XB
    whole = lambda shape: pl.BlockSpec(shape, lambda i: (0,) * len(shape))
    return pl.pallas_call(
        columns_kernel,
        grid=(steps,),
        out_shape=jax.ShapeDtypeStruct(state.shape, f32),
        in_specs=[
            pl.BlockSpec((XB, tile_y, width), lambda i: (i, 0, 0)),
            pl.BlockSpec((1, tile_y, width), lambda i: (jnp.maximum(XB * i - 1, 0), 0, 0)),
            pl.BlockSpec((1, tile_y, width), lambda i: (jnp.minimum(XB * i + XB, tile_x - 1), 0, 0)),
            whole(x_low.shape),
            whole(x_high.shape),
            pl.BlockSpec((XB, 1, width), lambda i: (i, 0, 0)),
            pl.BlockSpec((XB, 1, width), lambda i: (i, 0, 0)),
            whole(lat.shape),
            whole(count.shape),
            pl.BlockSpec((XB, tile_y, diffusion.shape[2]), lambda i: (i, 0, 0)),
            whole(scale.shape),
            pl.BlockSpec((32, XB * tile_y), lambda i: (0, i)),
            whole(left.shape),
            whole(right.shape),
            whole(stoich_t.shape),
        ],
        out_specs=pl.BlockSpec((XB, tile_y, width), lambda i: (i, 0, 0)),
        scratch_shapes=[
            pltpu.VMEM((256, 256), bf16),
            pltpu.VMEM((256, 256), bf16),
            pltpu.VMEM((256, 256), bf16),
            pltpu.VMEM((256, 128), bf16),
            pltpu.VMEM((steps, 32, 128), f32),
            pltpu.VMEM((steps, 32, 128), f32),
            pltpu.VMEM((32, 128), f32),
            pltpu.VMEM((width, XB * tile_y), f32),
            pltpu.VMEM((width, XB * tile_y), f32),
            pltpu.VMEM((64, XB * tile_y), f32),
        ],
        compiler_params=pltpu.CompilerParams(vmem_limit_bytes=56 << 20),
        name="columns",
    )(state, state, state, x_low, x_high, y_low, y_high, lat, count, diffusion, scale, source, left, right, stoich_t)


def body(
    state,
    lat_coef,
    diffusion,
    layer_count,
    species_scale,
    stream,
    reach_owner,
    reach_local,
    exch_coef,
    rate_left,
    rate_right,
    stoich,
):
    peers = lax.axis_size("gx") * lax.axis_size("gy")
    stream_t = stream.T
    flat, msg = pack(
        reach_owner.reshape(-1, 128), reach_local.reshape(-1, 128), exch_coef.reshape(-1, 128), stream_t, peers
    )
    source, back, x_low, x_high, y_low, y_high = exchange(msg, state)
    state_out = columns(
        state, x_low, x_high, y_low, y_high, lat_coef, layer_count, diffusion, species_scale[None, :], source,
        rate_left, rate_right, stoich.T,
    )
    stream_out = unpack(flat, back, stream_t).T
    return (state_out, stream_out)


def solution(mesh):
    return jax.shard_map(
        body,
        mesh=mesh,
        in_specs=(
            P("gx", "gy", None),
            P("gx", "gy"),
            P("gx", "gy", None),
            P("gx", "gy"),
            P(),
            P(("gx", "gy"), None),
            P(("gx", "gy"), None),
            P(("gx", "gy")),
            P(("gx", "gy")),
            P(),
            P(),
            P(),
        ),
        out_specs=(P("gx", "gy", None), P(("gx", "gy"), None)),
        check_vma=False,
    )
```

```python
import functools

import jax
import jax.numpy as jnp
from jax import lax
from jax.experimental import pallas as pl
from jax.experimental.pallas import tpu as pltpu
from jax.sharding import PartitionSpec as P

MESH = pl.DeviceIdType.MESH
f32, bf16, i32 = jnp.float32, jnp.bfloat16, jnp.int32
VM = pl.BlockSpec(memory_space=pltpu.VMEM)
ANY = pl.BlockSpec(memory_space=pl.ANY)

CAP = 64
ROWS = 16
MSG = ROWS + 1
FORM = 16
BATCH = 16


def iota(shape, dim):
    return lax.broadcasted_iota(i32, shape, dim)


def split(x):
    hi = x.astype(bf16)
    return hi, (x - hi.astype(f32)).astype(bf16)


def dot(a, b):
    return jnp.dot(a, b, preferred_element_type=f32)


def pack_kernel(owner, local, coef, stream_t, flat_out, msg, rows, buf, flat_v, flat_s, sem):
    groups = owner.shape[0]
    peers = msg.shape[0]
    sub, lane = iota((128, 128), 0), iota((128, 128), 1)
    upto = (sub <= lane).astype(bf16)
    ones = jnp.ones((128, 128), bf16)
    carry = jnp.zeros((128, 128), f32)
    for g in range(groups):
        mine = sub == owner[g : g + 1, :]
        onehot = mine.astype(f32).astype(bf16)
        count = dot(onehot, upto) + carry
        carry = carry + dot(onehot, ones)
        rank = jnp.sum(jnp.where(mine, count, 0.0), axis=0, keepdims=True)
        flat_v[g : g + 1, :] = owner[g : g + 1, :] * CAP + rank.astype(i32) - 1
    pltpu.make_async_copy(flat_v, flat_s, sem).start()
    flat_out[...] = flat_v[...]

    def fill(g, _):
        at = pl.multiple_of(g * 128, 128)
        block = jnp.concatenate(
            [
                stream_t[:, pl.ds(at, 128)],
                local[pl.ds(g, 1), :].astype(f32),
                coef[pl.ds(g, 1), :],
                jnp.zeros((94, 128), f32),
            ],
            axis=0,
        )
        rows[pl.ds(at, 128), :] = block.T
        return 0

    lax.fori_loop(0, groups, fill, 0)
    empty = jnp.where(lane == 32, -1.0, 0.0)

    def clear(g, _):
        buf[pl.ds(pl.multiple_of(g * 128, 128), 128), :] = empty
        return 0

    lax.fori_loop(0, buf.shape[0] // 128, clear, 0)
    pltpu.make_async_copy(flat_v, flat_s, sem).wait()

    def move(g, _):
        for j in range(128):
            buf[pl.ds(flat_s[g, j], 1), :] = rows[pl.ds(g * 128 + j, 1), :]
        return 0

    lax.fori_loop(0, groups, move, 0)
    lanes = iota((FORM * 16, 128), 1)
    spot = lanes // 8 == (16 - iota((FORM * 16, 128), 0) % 16) % 16

    def form(t, _):
        at = pl.multiple_of(t * FORM * CAP, FORM * CAP)
        part = buf[pl.ds(at, FORM * CAP), :].reshape(FORM, 4, 16, 128)
        part = [part[:, q].reshape(FORM * 16, 128) for q in range(4)]
        vals = pltpu.roll(part[3], 96, axis=1)
        for q in (2, 1):
            vals = jnp.where(lanes < 32 * (q + 1), pltpu.roll(part[q], 32 * q, axis=1), vals)
        vals = jnp.where(lanes < 32, part[0], vals)
        meta = jnp.zeros((FORM * 16, 128), f32)
        for q in range(4):
            moved = pltpu.roll(part[q], (96 + 2 * q) % 128, axis=1)
            meta = jnp.where((lanes >= 2 * q) & (lanes < 2 * q + 2), moved, meta)
        for shift in (8, 16, 32, 64):
            meta = meta + pltpu.roll(meta, shift, axis=1)
        meta = jnp.sum(jnp.where(spot, meta, 0.0).reshape(FORM, 16, 128), axis=1)
        to = pl.ds(pl.multiple_of(t * FORM, FORM), FORM)
        msg[to, pl.ds(0, ROWS), :] = vals.reshape(FORM, 16, 128)
        msg[to, pl.ds(ROWS, 1), :] = meta[:, None, :]
        return 0

    lax.fori_loop(0, peers // FORM, form, 0)


def pack(owner, local, coef, stream_t, peers):
    groups = owner.shape[0]
    return pl.pallas_call(
        pack_kernel,
        out_shape=(
            jax.ShapeDtypeStruct((groups, 128), i32),
            jax.ShapeDtypeStruct((peers, MSG, 128), f32),
        ),
        in_specs=[VM] * 4,
        out_specs=(VM, VM),
        scratch_shapes=[
            pltpu.VMEM((groups * 128, 128), f32),
            pltpu.VMEM((peers * CAP, 128), f32),
            pltpu.VMEM((groups, 128), i32),
            pltpu.SMEM((groups, 128), i32),
            pltpu.SemaphoreType.DMA,
        ],
        compiler_params=pltpu.CompilerParams(vmem_limit_bytes=48 << 20),
        name="pack",
    )(owner, local, coef, stream_t)


def flux_of(messages, top, acc, put):
    count = len(messages)
    rows = count * ROWS
    lane = iota((rows, 128), 1)
    lane_f, place, side = lane.astype(f32), lane // 32, (lane // 64).astype(f32)
    vals = jnp.concatenate([m[0:ROWS, :] for m in messages], axis=0)
    meta = jnp.concatenate(
        [
            pltpu.roll(jnp.broadcast_to(m[ROWS : ROWS + 1, :], (ROWS, 128)), 0, axis=1, stride=8, stride_axis=0)
            for m in messages
        ],
        axis=0,
    )

    def by_place(parts):
        out = parts[3]
        for q in (2, 1, 0):
            out = jnp.where(place == q, parts[q], out)
        return out

    onehots, parts, coefs = [], [], []
    for q in range(4):
        column = jnp.broadcast_to(meta[:, 2 * q : 2 * q + 1], (rows, 128))
        part = jnp.floor(column * (1.0 / 256.0))
        low = column - 256.0 * part
        onehots.append(
            jnp.concatenate(
                [jnp.where(low == lane_f + 128.0 * b, 1.0, 0.0).astype(bf16) for b in range(2)], axis=1
            )
        )
        parts.append(part)
        coefs.append(jnp.broadcast_to(meta[:, 2 * q + 1 : 2 * q + 2], (rows, 128)))
    onehot = jnp.concatenate(onehots, axis=0)
    picked = dot(onehot, top[...])
    tops = []
    for q in range(4):
        p = picked[rows * q : rows * q + rows, :]
        p = jnp.where(parts[q] == side, p[:, 0:128], 0.0) + jnp.where(parts[q] == side + 2.0, p[:, 128:256], 0.0)
        p = p + pltpu.roll(p, 64, axis=1)
        tops.append(p + pltpu.roll(p, 32, axis=1))
    flux = by_place(coefs) * (vals - by_place(tops))
    for p in range(count):
        put(p, flux[ROWS * p : ROWS * p + ROWS, :])
    flux_t, part_t = flux.T, by_place(parts).T
    flux_t = jnp.concatenate([flux_t[32 * q : 32 * q + 32, :] for q in range(4)], axis=1)
    part_t = jnp.concatenate([part_t[32 * q : 32 * q + 1, :] for q in range(4)], axis=1)
    high = flux_t.astype(bf16).astype(f32)
    both = jnp.concatenate([high, flux_t - high], axis=0)
    spread = jnp.concatenate([jnp.where(part_t == float(g), both, 0.0).astype(bf16) for g in range(4)], axis=0)
    acc[...] += dot(spread, onehot)


def top_of(state_top, top):
    lane = iota((256, 128), 1)
    quarters = []
    for g in range(4):
        t = jnp.where(lane < 32, state_top[256 * g : 256 * g + 256, :], 0.0)
        high = t.astype(bf16).astype(f32)
        quarters.append(high + pltpu.roll(t - high, 32, axis=1))
    top[...] = jnp.concatenate(
        [quarters[g] + pltpu.roll(quarters[g + 1], 64, axis=1) for g in (0, 2)], axis=1
    ).astype(bf16)


def source_of(acc, source):
    for g in range(4):
        source[:, 256 * g : 256 * g + 256] = acc[64 * g : 64 * g + 32, :] + acc[64 * g + 32 : 64 * g + 64, :]


def prepare(st, y_low, y_high, lat_col, count, diff, rhs, iface):
    row = iota((32, 128), 0)

    def step(cb, _):
        block, lanes = cb // 2, pl.ds(pl.multiple_of(lax.rem(cb, 2) * 128, 128), 128)
        lats = [jnp.broadcast_to(lat_col[cb, :, x : x + 1], (32, 128)) for x in range(4)]
        for j in range(16):
            at = slice(128 * j, 128 * j + 128)
            parts = []
            for x in range(4):
                here = 4 * cb + x
                s = st[here + 1, :, at]
                lower = jnp.where(row == 0, y_low[here, :, at], pltpu.roll(s, 1, axis=0))
                upper = jnp.where(row == 31, y_high[here, :, at], pltpu.roll(s, 31, axis=0))
                beside = (st[here, :, at] + st[here + 2, :, at]) + (lower + upper)
                parts.append(s + lats[x] * (beside - 4.0 * s))
            rhs[block, at, lanes] = jnp.concatenate(parts, axis=0).T
        counts = jnp.concatenate([count[pl.ds(4 * cb + x, 1), :] for x in range(4)], axis=1)
        d = diff[pl.ds(4 * cb, 4)].reshape(128, 64)
        d = jnp.concatenate([d, jnp.zeros((128, 64), f32)], axis=1).T[0:64, :]
        iface[block, :, lanes] = jnp.where(iota((64, 128), 0) + 1 < counts, d, 0.0)
        return 0

    lax.fori_loop(0, 8, step, 0)


def eliminate(rhs, coef, iface, scale_col, block):
    scales = jnp.concatenate([scale_col[...]] * 4, axis=1)

    def cell(k):
        return pl.ds(32 * k, 32)

    def put(ref, k, value):
        ref[block, cell(k), :] = value[:, 0:256]
        ref[block + 1, cell(k), :] = value[:, 256:512]

    def get(k):
        return jnp.concatenate([rhs[block, cell(k), :], rhs[block + 1, cell(k), :]], axis=1)

    def layers(n, carry):
        c, d, u = carry
        for m in range(7):
            k = 63 - 7 * n - m
            v = scales * jnp.concatenate([iface[block, pl.ds(k - 1, 1), :], iface[block + 1, pl.ds(k - 1, 1), :]], axis=1)
            r = 1.0 / (1.0 + v + u * (1.0 - c))
            d = (get(k) + u * d) * r
            c = v * r
            u = v
            put(rhs, k, d)
            put(coef, k, c)
        return c, d, u

    zero = jnp.zeros((32, 512), f32)
    c, d, u = lax.fori_loop(0, 9, layers, (zero, zero, zero))
    r = 1.0 / (1.0 + u * (1.0 - c))
    put(rhs, 0, (get(0) + u * d) * r)
    put(coef, 0, r)


def exchange_kernel(
    msg, state, lat, count, diff, scale, source, back, rhs_out, coef_out,
    st, y_low, y_high, rhs, coef, iface, lat_col, scale_col, inbox, outbox, top, acc,
    send1, recv1, send2, recv2, send_edge, recv_edge, local,
):
    peers = msg.shape[0]
    size_x, size_y = lax.axis_size("gx"), lax.axis_size("gy")
    gx, gy = lax.axis_index("gx"), lax.axis_index("gy")
    me = gx * size_y + gy
    tile_x, tile_y, _ = state.shape

    def device(t):
        return (t // size_y, lax.rem(t, size_y))

    barrier = pltpu.get_barrier_semaphore()

    def greet(d, _):
        pl.semaphore_signal(barrier, inc=1, device_id=device(lax.rem(me + d, peers)), device_id_type=MESH)
        return 0

    lax.fori_loop(1, peers, greet, 0)
    load = pltpu.make_async_copy(state, st.at[pl.ds(1, tile_x)], local.at[0])
    load.start()

    edges = [
        (state.at[pl.ds(tile_x - 1, 1)], st.at[pl.ds(0, 1)], (lax.rem(gx + 1, size_x), gy), gx < size_x - 1, gx > 0),
        (state.at[pl.ds(0, 1)], st.at[pl.ds(tile_x + 1, 1)], (lax.rem(gx + size_x - 1, size_x), gy), gx > 0, gx < size_x - 1),
        (state.at[:, pl.ds(tile_y - 1, 1)], y_low, (gx, lax.rem(gy + 1, size_y)), gy < size_y - 1, gy > 0),
        (state.at[:, pl.ds(0, 1)], y_high, (gx, lax.rem(gy + size_y - 1, size_y)), gy > 0, gy < size_y - 1),
    ]

    def edge(n):
        block, to, device_id, _, _ = edges[n]
        return pltpu.make_async_remote_copy(
            src_ref=block,
            dst_ref=to,
            send_sem=send_edge.at[n],
            recv_sem=recv_edge.at[n],
            device_id=device_id,
            device_id_type=MESH,
        )

    for n in range(4):
        @pl.when(jnp.logical_not(edges[n][4]))
        def _():
            edges[n][1][...] = jnp.zeros(edges[n][1].shape, f32)

    def send(d):
        to = lax.rem(me + d, peers)
        return pltpu.make_async_remote_copy(
            src_ref=msg.at[to],
            dst_ref=inbox.at[d],
            send_sem=send1,
            recv_sem=recv1.at[d],
            device_id=device(to),
            device_id_type=MESH,
        )

    def reply(d):
        to = lax.rem(me + peers - d, peers)
        return pltpu.make_async_remote_copy(
            src_ref=outbox.at[d],
            dst_ref=back.at[me],
            send_sem=send2,
            recv_sem=recv2,
            device_id=device(to),
            device_id_type=MESH,
        )

    def start(d, _):
        send(d).start()
        return 0

    pl.semaphore_wait(barrier, peers - 1)
    for n in range(4):
        pl.when(edges[n][3])(edge(n).start)
    lax.fori_loop(1, peers, start, 0)
    keep = pltpu.make_async_copy(msg.at[me], inbox.at[0], recv1.at[0])
    keep.start()

    lat_t = jnp.concatenate([lat[...], jnp.zeros((32, 96), f32)], axis=1)
    lat_t = jnp.concatenate([lat_t, jnp.zeros((96, 128), f32)], axis=0).T
    for g in range(8):
        lat_col[g] = pltpu.roll(lat_t, (128 - 4 * g) % 128, axis=1)[0:32, :]
    scale_col[...] = jnp.broadcast_to(
        jnp.sum(
            jnp.where(iota((32, 32), 0) == iota((32, 32), 1), jnp.broadcast_to(scale[...], (32, 32)), 0.0),
            axis=1,
            keepdims=True,
        ),
        (32, 128),
    )
    acc[...] = jnp.zeros_like(acc)
    load.wait()
    top_of(st[1 : tile_x + 1, :, 0:128].reshape(tile_x * tile_y, 128), top)
    for n in range(4):
        pl.when(edges[n][4])(edge(n).wait_recv)
    prepare(st, y_low, y_high, lat_col, count, diff, rhs, iface)
    saved = []
    for block in (0, 2):
        eliminate(rhs, coef, iface, scale_col, block)
        for n, (made, to) in enumerate(((rhs, rhs_out), (coef, coef_out))):
            two = pl.ds(block, 2)
            saved.append(pltpu.make_async_copy(made.at[two], to.at[two], local.at[1 + block + n]))
            saved[-1].start()
    keep.wait()

    def work(c, first):
        for p in range(BATCH):
            if not (first and p == 0):
                send(c * BATCH + p).wait_recv()

        def put(p, value):
            outbox[pl.ds(c * BATCH + p, 1)] = value[None]

        flux_of([inbox[c * BATCH + p] for p in range(BATCH)], top, acc, put)
        for p in range(BATCH):
            if not (first and p == 0):
                reply(c * BATCH + p).start()

    work(0, True)

    def step(c, _):
        work(c, False)
        return 0

    lax.fori_loop(1, peers // BATCH, step, 0)
    own = pltpu.make_async_copy(outbox.at[0], back.at[me], recv1.at[0])
    own.start()
    source_of(acc, source)
    own.wait()
    for n in range(4):
        pl.when(edges[n][3])(edge(n).wait_send)
    for copy in saved:
        copy.wait()
    rest = pl.ds(0, peers - 1)
    pltpu.make_async_copy(msg.at[rest], msg.at[rest], send1).wait()
    pltpu.make_async_copy(outbox.at[rest], outbox.at[rest], send2).wait()
    pltpu.make_async_copy(back.at[rest], back.at[rest], recv2).wait()


def exchange(msg, state, lat, count, diffusion, scale):
    peers = msg.shape[0]
    tile_x, tile_y, width = state.shape
    solve = jax.ShapeDtypeStruct((4, width, 256), f32)
    return pl.pallas_call(
        exchange_kernel,
        out_shape=(
            jax.ShapeDtypeStruct((32, tile_x * tile_y), f32),
            jax.ShapeDtypeStruct((peers, ROWS, 128), f32),
            solve,
            solve,
        ),
        in_specs=[ANY, ANY, VM, VM, VM, VM],
        out_specs=(VM, ANY, ANY, ANY),
        scratch_shapes=[
            pltpu.VMEM((tile_x + 2, tile_y, width), f32),
            pltpu.VMEM((tile_x, 1, width), f32),
            pltpu.VMEM((tile_x, 1, width), f32),
            pltpu.VMEM((4, width, 256), f32),
            pltpu.VMEM((4, width, 256), f32),
            pltpu.VMEM((4, 64, 256), f32),
            pltpu.VMEM((8, 32, 128), f32),
            pltpu.VMEM((32, 128), f32),
            pltpu.VMEM((peers, MSG, 128), f32),
            pltpu.VMEM((peers, ROWS, 128), f32),
            pltpu.VMEM((256, 256), bf16),
            pltpu.VMEM((256, 256), f32),
            pltpu.SemaphoreType.DMA,
            pltpu.SemaphoreType.DMA((peers,)),
            pltpu.SemaphoreType.DMA,
            pltpu.SemaphoreType.DMA,
            pltpu.SemaphoreType.DMA((4,)),
            pltpu.SemaphoreType.DMA((4,)),
            pltpu.SemaphoreType.DMA((5,)),
        ],
        compiler_params=pltpu.CompilerParams(collective_id=0, has_side_effects=True, vmem_limit_bytes=58 << 20),
        name="exchange",
    )(msg, state, lat, count, diffusion, scale)


def unpack_kernel(flat, back, stream_t, out, buf, rows):
    groups = flat.shape[0]
    peers = back.shape[0]

    def spread(t, _):
        m = back[pl.ds(pl.multiple_of(t * FORM, FORM), FORM)].reshape(FORM * 16, 128)
        parts = [m] + [pltpu.roll(m, 128 - 32 * q, axis=1) for q in range(1, 4)]
        parts = [p.reshape(FORM, 1, 16, 128) for p in parts]
        at = pl.multiple_of(t * FORM * CAP, FORM * CAP)
        buf[pl.ds(at, FORM * CAP), :] = jnp.concatenate(parts, axis=1).reshape(FORM * CAP, 128)
        return 0

    lax.fori_loop(0, peers // FORM, spread, 0)

    def move(g, _):
        at = pl.multiple_of(g * 128, 128)
        for j in range(128):
            rows[pl.ds(j, 1), :] = buf[pl.ds(flat[g, j], 1), :]
        out[:, pl.ds(at, 128)] = stream_t[:, pl.ds(at, 128)] - 0.5 * rows[...].T[0:32, :]
        return 0

    lax.fori_loop(0, groups, move, 0)


def unpack(flat, back, stream_t):
    peers = back.shape[0]
    return pl.pallas_call(
        unpack_kernel,
        out_shape=jax.ShapeDtypeStruct(stream_t.shape, f32),
        in_specs=[pl.BlockSpec(memory_space=pltpu.SMEM), VM, VM],
        out_specs=VM,
        scratch_shapes=[pltpu.VMEM((peers * CAP, 128), f32), pltpu.VMEM((128, 128), f32)],
        compiler_params=pltpu.CompilerParams(vmem_limit_bytes=48 << 20),
        name="unpack",
    )(flat, back, stream_t)


XB = 8
PART = 8


def columns_kernel(rhs, coef, count, source, left, right, stoich_t, out, w_a, w_b, s_both, s_high, count_col, solved_t):
    i = pl.program_id(0)
    lane = iota((128, 128), 1)

    @pl.when(i == 0)
    def _():
        inside = iota((64, 128), 0) // 32 == iota((64, 128), 1) // 64

        def spread(w):
            return jnp.where(inside, jnp.concatenate([jnp.concatenate([w] * 2, axis=1)] * 2, axis=0), 0.0)

        pair = jnp.concatenate([spread(left[...]), spread(right[...])], axis=1)
        high, low = split(pair)
        none = jnp.zeros((64, 256), bf16)
        w_a[...] = jnp.concatenate([high, high, low, none], axis=0)
        w_b[...] = jnp.concatenate([high, high, none, low], axis=0)
        inside = iota((128, 256), 0) // 32 == iota((128, 256), 1) // 64
        wide = jnp.concatenate([stoich_t[...]] * 4, axis=1)
        high, low = split(jnp.where(inside, jnp.concatenate([wide] * 4, axis=0), 0.0).T)
        s_both[...] = jnp.concatenate([high, low], axis=1)
        s_high[...] = high
        turned = jnp.concatenate([count[...].astype(f32), jnp.zeros((32, 96), f32)], axis=1)
        turned = jnp.concatenate([turned, jnp.zeros((96, 128), f32)], axis=0).T
        for g in range(4):
            count_col[g] = pltpu.roll(turned, (128 - XB * g) % 128, axis=1)[0:32, :]

    x = rhs[0, 0:32, :] + coef[0, 0:32, :] * source[...]
    solved_t[0:32, :] = x
    for k in range(1, 64):
        cell = slice(32 * k, 32 * k + 32)
        x = rhs[0, cell, :] + coef[0, cell, :] * x
        solved_t[cell, :] = x

    half = lane < 64
    for cb in range(2):
        counts = jnp.concatenate(
            [jnp.broadcast_to(count_col[i, :, x : x + 1], (32, 128)) for x in range(4 * cb, 4 * cb + 4)], axis=0
        )
        depth = counts - (lane // 32).astype(f32)
        for first in range(0, 16, PART):
            solved, pair_a, pair_b = [], [], []
            for j in range(first, first + PART):
                x = solved_t[128 * j : 128 * j + 128, 128 * cb : 128 * cb + 128].T
                high = x.astype(bf16)
                wide = high.astype(f32)
                low = pltpu.roll(x - wide, 64, axis=1)
                pair_a.append(jnp.concatenate([jnp.where(half, wide, low).astype(bf16), high], axis=1))
                pair_b.append(jnp.concatenate([jnp.where(half, low, wide).astype(bf16), high], axis=1))
                solved.append(x)
            both = dot(jnp.concatenate(pair_a, axis=0), w_a[...])
            rates_a = split(both[:, 0:128] * both[:, 128:256])
            both = dot(jnp.concatenate(pair_b, axis=0), w_b[...])
            rates_b = split(both[:, 0:128] * both[:, 128:256])
            change = dot(jnp.concatenate([rates_a[0], rates_b[0]], axis=1), s_both[...])
            change = change[:, 0:128] + change[:, 128:256]
            change = change + dot(jnp.concatenate([rates_a[1], rates_b[1]], axis=1), s_high[...])
            for n in range(PART):
                j = first + n
                new = solved[n] + jnp.where(depth > 4.0 * j, 0.1, 0.0) * change[128 * n : 128 * n + 128, :]
                for p in range(4):
                    out[4 * cb + p, :, 128 * j : 128 * j + 128] = new[32 * p : 32 * p + 32, :]


def columns(rhs, coef, count, source, left, right, stoich_t):
    tile_x, tile_y = count.shape
    steps, width, _ = rhs.shape
    whole = lambda shape: pl.BlockSpec(shape, lambda i: (0,) * len(shape))
    return pl.pallas_call(
        columns_kernel,
        grid=(steps,),
        out_shape=jax.ShapeDtypeStruct((tile_x, tile_y, width), f32),
        in_specs=[
            pl.BlockSpec((1, width, 256), lambda i: (i, 0, 0)),
            pl.BlockSpec((1, width, 256), lambda i: (i, 0, 0)),
            whole(count.shape),
            pl.BlockSpec((32, 256), lambda i: (0, i)),
            whole(left.shape),
            whole(right.shape),
            whole(stoich_t.shape),
        ],
        out_specs=pl.BlockSpec((XB, tile_y, width), lambda i: (i, 0, 0)),
        scratch_shapes=[
            pltpu.VMEM((256, 256), bf16),
            pltpu.VMEM((256, 256), bf16),
            pltpu.VMEM((256, 256), bf16),
            pltpu.VMEM((256, 128), bf16),
            pltpu.VMEM((steps, 32, 128), f32),
            pltpu.VMEM((width, 256), f32),
        ],
        compiler_params=pltpu.CompilerParams(vmem_limit_bytes=56 << 20),
        name="columns",
    )(rhs, coef, count, source, left, right, stoich_t)


def body(
    state,
    lat_coef,
    diffusion,
    layer_count,
    species_scale,
    stream,
    reach_owner,
    reach_local,
    exch_coef,
    rate_left,
    rate_right,
    stoich,
):
    peers = lax.axis_size("gx") * lax.axis_size("gy")
    stream_t = stream.T
    flat, msg = pack(
        reach_owner.reshape(-1, 128), reach_local.reshape(-1, 128), exch_coef.reshape(-1, 128), stream_t, peers
    )
    source, back, rhs, coef = exchange(msg, state, lat_coef, layer_count, diffusion, species_scale[None, :])
    state_out = columns(rhs, coef, layer_count, source, rate_left, rate_right, stoich.T)
    stream_out = unpack(flat, back, stream_t).T
    return (state_out, stream_out)


def solution(mesh):
    return jax.shard_map(
        body,
        mesh=mesh,
        in_specs=(
            P("gx", "gy", None),
            P("gx", "gy"),
            P("gx", "gy", None),
            P("gx", "gy"),
            P(),
            P(("gx", "gy"), None),
            P(("gx", "gy"), None),
            P(("gx", "gy")),
            P(("gx", "gy")),
            P(),
            P(),
            P(),
        ),
        out_specs=(P("gx", "gy", None), P(("gx", "gy"), None)),
        check_vma=False,
    )
```

```python
import functools

import jax
import jax.numpy as jnp
from jax import lax
from jax.experimental import pallas as pl
from jax.experimental.pallas import tpu as pltpu
from jax.sharding import PartitionSpec as P

MESH = pl.DeviceIdType.MESH
f32, bf16, i32 = jnp.float32, jnp.bfloat16, jnp.int32
VM = pl.BlockSpec(memory_space=pltpu.VMEM)
ANY = pl.BlockSpec(memory_space=pl.ANY)

CAP = 64
ROWS = 16
MSG = ROWS + 1
FORM = 16
BATCH = 16


def iota(shape, dim):
    return lax.broadcasted_iota(i32, shape, dim)


def split(x):
    hi = x.astype(bf16)
    return hi, (x - hi.astype(f32)).astype(bf16)


def dot(a, b):
    return jnp.dot(a, b, preferred_element_type=f32)


def pack_kernel(owner, local, coef, stream_t, flat_out, msg, rows, buf, flat_v, flat_s, sem):
    groups = owner.shape[0]
    peers = msg.shape[0]
    sub, lane = iota((128, 128), 0), iota((128, 128), 1)
    upto = (sub <= lane).astype(bf16)
    ones = jnp.ones((128, 128), bf16)
    carry = jnp.zeros((128, 128), f32)
    for g in range(groups):
        mine = sub == owner[g : g + 1, :]
        onehot = mine.astype(f32).astype(bf16)
        count = dot(onehot, upto) + carry
        carry = carry + dot(onehot, ones)
        rank = jnp.sum(jnp.where(mine, count, 0.0), axis=0, keepdims=True)
        flat_v[g : g + 1, :] = owner[g : g + 1, :] * CAP + rank.astype(i32) - 1
    pltpu.make_async_copy(flat_v, flat_s, sem).start()
    flat_out[...] = flat_v[...]

    def fill(g, _):
        at = pl.multiple_of(g * 128, 128)
        block = jnp.concatenate(
            [
                stream_t[:, pl.ds(at, 128)],
                local[pl.ds(g, 1), :].astype(f32),
                coef[pl.ds(g, 1), :],
                jnp.zeros((94, 128), f32),
            ],
            axis=0,
        )
        rows[pl.ds(at, 128), :] = block.T
        return 0

    lax.fori_loop(0, groups, fill, 0)
    empty = jnp.where(lane == 32, -1.0, 0.0)

    def clear(g, _):
        buf[pl.ds(pl.multiple_of(g * 128, 128), 128), :] = empty
        return 0

    lax.fori_loop(0, buf.shape[0] // 128, clear, 0)
    pltpu.make_async_copy(flat_v, flat_s, sem).wait()

    def move(g, _):
        for j in range(128):
            buf[pl.ds(flat_s[g, j], 1), :] = rows[pl.ds(g * 128 + j, 1), :]
        return 0

    lax.fori_loop(0, groups, move, 0)
    lanes = iota((FORM * 16, 128), 1)
    spot = lanes // 8 == (16 - iota((FORM * 16, 128), 0) % 16) % 16

    def form(t, _):
        at = pl.multiple_of(t * FORM * CAP, FORM * CAP)
        part = buf[pl.ds(at, FORM * CAP), :].reshape(FORM, 4, 16, 128)
        part = [part[:, q].reshape(FORM * 16, 128) for q in range(4)]
        vals = pltpu.roll(part[3], 96, axis=1)
        for q in (2, 1):
            vals = jnp.where(lanes < 32 * (q + 1), pltpu.roll(part[q], 32 * q, axis=1), vals)
        vals = jnp.where(lanes < 32, part[0], vals)
        meta = jnp.zeros((FORM * 16, 128), f32)
        for q in range(4):
            moved = pltpu.roll(part[q], (96 + 2 * q) % 128, axis=1)
            meta = jnp.where((lanes >= 2 * q) & (lanes < 2 * q + 2), moved, meta)
        for shift in (8, 16, 32, 64):
            meta = meta + pltpu.roll(meta, shift, axis=1)
        meta = jnp.sum(jnp.where(spot, meta, 0.0).reshape(FORM, 16, 128), axis=1)
        to = pl.ds(pl.multiple_of(t * FORM, FORM), FORM)
        msg[to, pl.ds(0, ROWS), :] = vals.reshape(FORM, 16, 128)
        msg[to, pl.ds(ROWS, 1), :] = meta[:, None, :]
        return 0

    lax.fori_loop(0, peers // FORM, form, 0)


def pack(owner, local, coef, stream_t, peers):
    groups = owner.shape[0]
    return pl.pallas_call(
        pack_kernel,
        out_shape=(
            jax.ShapeDtypeStruct((groups, 128), i32),
            jax.ShapeDtypeStruct((peers, MSG, 128), f32),
        ),
        in_specs=[VM] * 4,
        out_specs=(VM, VM),
        scratch_shapes=[
            pltpu.VMEM((groups * 128, 128), f32),
            pltpu.VMEM((peers * CAP, 128), f32),
            pltpu.VMEM((groups, 128), i32),
            pltpu.SMEM((groups, 128), i32),
            pltpu.SemaphoreType.DMA,
        ],
        compiler_params=pltpu.CompilerParams(vmem_limit_bytes=48 << 20),
        name="pack",
    )(owner, local, coef, stream_t)


def flux_of(messages, top, acc, put):
    count = len(messages)
    rows = count * ROWS
    lane = iota((rows, 128), 1)
    lane_f, place, side = lane.astype(f32), lane // 32, (lane // 64).astype(f32)
    vals = jnp.concatenate([m[0:ROWS, :] for m in messages], axis=0)
    meta = jnp.concatenate(
        [
            pltpu.roll(jnp.broadcast_to(m[ROWS : ROWS + 1, :], (ROWS, 128)), 0, axis=1, stride=8, stride_axis=0)
            for m in messages
        ],
        axis=0,
    )

    def by_place(parts):
        out = parts[3]
        for q in (2, 1, 0):
            out = jnp.where(place == q, parts[q], out)
        return out

    onehots, parts, coefs = [], [], []
    for q in range(4):
        column = jnp.broadcast_to(meta[:, 2 * q : 2 * q + 1], (rows, 128))
        part = jnp.floor(column * (1.0 / 256.0))
        low = column - 256.0 * part
        onehots.append(
            jnp.concatenate(
                [jnp.where(low == lane_f + 128.0 * b, 1.0, 0.0).astype(bf16) for b in range(2)], axis=1
            )
        )
        parts.append(part)
        coefs.append(jnp.broadcast_to(meta[:, 2 * q + 1 : 2 * q + 2], (rows, 128)))
    onehot = jnp.concatenate(onehots, axis=0)
    picked = dot(onehot, top[...])
    tops = []
    for q in range(4):
        p = picked[rows * q : rows * q + rows, :]
        p = jnp.where(parts[q] == side, p[:, 0:128], 0.0) + jnp.where(parts[q] == side + 2.0, p[:, 128:256], 0.0)
        p = p + pltpu.roll(p, 64, axis=1)
        tops.append(p + pltpu.roll(p, 32, axis=1))
    flux = by_place(coefs) * (vals - by_place(tops))
    for p in range(count):
        put(p, flux[ROWS * p : ROWS * p + ROWS, :])
    flux_t, part_t = flux.T, by_place(parts).T
    flux_t = jnp.concatenate([flux_t[32 * q : 32 * q + 32, :] for q in range(4)], axis=1)
    part_t = jnp.concatenate([part_t[32 * q : 32 * q + 1, :] for q in range(4)], axis=1)
    high = flux_t.astype(bf16).astype(f32)
    both = jnp.concatenate([high, flux_t - high], axis=0)
    spread = jnp.concatenate([jnp.where(part_t == float(g), both, 0.0).astype(bf16) for g in range(4)], axis=0)
    acc[...] += dot(spread, onehot)


def top_of(state_top, top):
    lane = iota((256, 128), 1)
    quarters = []
    for g in range(4):
        t = jnp.where(lane < 32, state_top[256 * g : 256 * g + 256, :], 0.0)
        high = t.astype(bf16).astype(f32)
        quarters.append(high + pltpu.roll(t - high, 32, axis=1))
    top[...] = jnp.concatenate(
        [quarters[g] + pltpu.roll(quarters[g + 1], 64, axis=1) for g in (0, 2)], axis=1
    ).astype(bf16)


def prepare(st, y_in, lat_col, count, diff, rhs, iface):
    row = iota((32, 128), 0)

    def step(cb, _):
        block, lanes = cb // 2, pl.ds(pl.multiple_of(lax.rem(cb, 2) * 128, 128), 128)
        lats = [jnp.broadcast_to(lat_col[cb, :, x : x + 1], (32, 128)) for x in range(4)]
        for j in range(16):
            at = slice(128 * j, 128 * j + 128)
            parts = []
            for x in range(4):
                here = 4 * cb + x
                s = st[here + 1, :, at]
                lower = jnp.where(row == 0, y_in[0, here, :, at], pltpu.roll(s, 1, axis=0))
                upper = jnp.where(row == 31, y_in[1, here, :, at], pltpu.roll(s, 31, axis=0))
                beside = (st[here, :, at] + st[here + 2, :, at]) + (lower + upper)
                parts.append(s + lats[x] * (beside - 4.0 * s))
            rhs[block, at, lanes] = jnp.concatenate(parts, axis=0).T
        counts = jnp.concatenate([count[pl.ds(4 * cb + x, 1), :] for x in range(4)], axis=1)
        d = diff[pl.ds(4 * cb, 4)].reshape(128, 64)
        d = jnp.concatenate([d, jnp.zeros((128, 64), f32)], axis=1).T[0:64, :]
        iface[block, :, lanes] = jnp.where(iota((64, 128), 0) + 1 < counts, d, 0.0)
        return 0

    lax.fori_loop(0, 8, step, 0)


def eliminate(rhs, coef, iface, scale_col, block):
    scales = jnp.concatenate([scale_col[...]] * 4, axis=1)

    def cell(k):
        return pl.ds(32 * k, 32)

    def put(ref, k, value):
        ref[block, cell(k), :] = value[:, 0:256]
        ref[block + 1, cell(k), :] = value[:, 256:512]

    def get(k):
        return jnp.concatenate([rhs[block, cell(k), :], rhs[block + 1, cell(k), :]], axis=1)

    def layers(n, carry):
        c, d, u = carry
        for m in range(7):
            k = 63 - 7 * n - m
            v = scales * jnp.concatenate([iface[block, pl.ds(k - 1, 1), :], iface[block + 1, pl.ds(k - 1, 1), :]], axis=1)
            r = 1.0 / (1.0 + v + u * (1.0 - c))
            d = (get(k) + u * d) * r
            c = v * r
            u = v
            put(rhs, k, d)
            put(coef, k, c)
        return c, d, u

    zero = jnp.zeros((32, 512), f32)
    c, d, u = lax.fori_loop(0, 9, layers, (zero, zero, zero))
    r = 1.0 / (1.0 + u * (1.0 - c))
    put(rhs, 0, (get(0) + u * d) * r)
    put(coef, 0, r)


PART = 8


def columns_last(a, out):
    a = jnp.concatenate([a, jnp.zeros((32, 96), f32)], axis=1)
    a = jnp.concatenate([a, jnp.zeros((96, 128), f32)], axis=0).T
    for g in range(8):
        out[g] = pltpu.roll(a, (128 - 4 * g) % 128, axis=1)[0:32, :]


def weights_of(left, right, stoich_t, w_a, w_b, s_both, s_high):
    inside = iota((64, 128), 0) // 32 == iota((64, 128), 1) // 64

    def spread(w):
        return jnp.where(inside, jnp.concatenate([jnp.concatenate([w] * 2, axis=1)] * 2, axis=0), 0.0)

    pair = jnp.concatenate([spread(left[...]), spread(right[...])], axis=1)
    high, low = split(pair)
    none = jnp.zeros((64, 256), bf16)
    w_a[...] = jnp.concatenate([high, high, low, none], axis=0)
    w_b[...] = jnp.concatenate([high, high, none, low], axis=0)
    inside = iota((128, 256), 0) // 32 == iota((128, 256), 1) // 64
    wide = jnp.concatenate([stoich_t[...]] * 4, axis=1)
    high, low = split(jnp.where(inside, jnp.concatenate([wide] * 4, axis=0), 0.0).T)
    s_both[...] = jnp.concatenate([high, low], axis=1)
    s_high[...] = high


def finish(rhs, coef, count_col, acc, w_a, w_b, s_both, s_high, solved_t, st, i):
    lane = iota((128, 128), 1)
    at = pl.multiple_of(64 * i, 64)
    source = acc[pl.ds(at, 32), :] + acc[pl.ds(at + 32, 32), :]
    x = rhs[i, 0:32, :] + coef[i, 0:32, :] * source
    solved_t[0:32, :] = x
    for k in range(1, 64):
        cell = slice(32 * k, 32 * k + 32)
        x = rhs[i, cell, :] + coef[i, cell, :] * x
        solved_t[cell, :] = x

    half = lane < 64
    for cb in range(2):
        counts = jnp.concatenate(
            [jnp.broadcast_to(count_col[2 * i + cb, :, x : x + 1], (32, 128)) for x in range(4)], axis=0
        )
        depth = counts - (lane // 32).astype(f32)
        for first in range(0, 16, PART):
            solved, pair_a, pair_b = [], [], []
            for j in range(first, first + PART):
                x = solved_t[128 * j : 128 * j + 128, 128 * cb : 128 * cb + 128].T
                high = x.astype(bf16)
                wide = high.astype(f32)
                low = pltpu.roll(x - wide, 64, axis=1)
                pair_a.append(jnp.concatenate([jnp.where(half, wide, low).astype(bf16), high], axis=1))
                pair_b.append(jnp.concatenate([jnp.where(half, low, wide).astype(bf16), high], axis=1))
                solved.append(x)
            both = dot(jnp.concatenate(pair_a, axis=0), w_a[...])
            rates_a = split(both[:, 0:128] * both[:, 128:256])
            both = dot(jnp.concatenate(pair_b, axis=0), w_b[...])
            rates_b = split(both[:, 0:128] * both[:, 128:256])
            change = dot(jnp.concatenate([rates_a[0], rates_b[0]], axis=1), s_both[...])
            change = change[:, 0:128] + change[:, 128:256]
            change = change + dot(jnp.concatenate([rates_a[1], rates_b[1]], axis=1), s_high[...])
            for n in range(PART):
                j = first + n
                new = solved[n] + jnp.where(depth > 4.0 * j, 0.1, 0.0) * change[128 * n : 128 * n + 128, :]
                for p in range(4):
                    st[8 * i + 4 * cb + p + 1, :, 128 * j : 128 * j + 128] = new[32 * p : 32 * p + 32, :]


def exchange_kernel(
    msg, state, lat, count, diff, scale, left, right, stoich_t, back, done,
    st, y_in, y_out, rhs, coef, iface, lat_col, count_col, scale_col, inbox, outbox, top, acc,
    w_a, w_b, s_both, s_high, solved_t,
    send1, recv1, send2, recv2, send_edge, recv_edge, local,
):
    peers = msg.shape[0]
    size_x, size_y = lax.axis_size("gx"), lax.axis_size("gy")
    gx, gy = lax.axis_index("gx"), lax.axis_index("gy")
    me = gx * size_y + gy
    tile_x, tile_y, _ = state.shape

    def device(t):
        return (t // size_y, lax.rem(t, size_y))

    barrier = pltpu.get_barrier_semaphore()

    def greet(d, _):
        pl.semaphore_signal(barrier, inc=1, device_id=device(lax.rem(me + d, peers)), device_id_type=MESH)
        return 0

    lax.fori_loop(1, peers, greet, 0)
    load = pltpu.make_async_copy(state, st.at[pl.ds(1, tile_x)], local.at[0])
    load.start()

    edges = [
        (state.at[pl.ds(tile_x - 1, 1)], st.at[pl.ds(0, 1)], (lax.rem(gx + 1, size_x), gy), gx < size_x - 1, gx > 0),
        (state.at[pl.ds(0, 1)], st.at[pl.ds(tile_x + 1, 1)], (lax.rem(gx + size_x - 1, size_x), gy), gx > 0, gx < size_x - 1),
        (y_out.at[0], y_in.at[0], (gx, lax.rem(gy + 1, size_y)), gy < size_y - 1, gy > 0),
        (y_out.at[1], y_in.at[1], (gx, lax.rem(gy + size_y - 1, size_y)), gy > 0, gy < size_y - 1),
    ]

    def edge(n):
        block, to, device_id, _, _ = edges[n]
        return pltpu.make_async_remote_copy(
            src_ref=block,
            dst_ref=to,
            send_sem=send_edge.at[n],
            recv_sem=recv_edge.at[n],
            device_id=device_id,
            device_id_type=MESH,
        )

    for n in range(4):
        @pl.when(jnp.logical_not(edges[n][4]))
        def _():
            edges[n][1][...] = jnp.zeros(edges[n][1].shape, f32)

    def send(d):
        to = lax.rem(me + d, peers)
        return pltpu.make_async_remote_copy(
            src_ref=msg.at[to],
            dst_ref=inbox.at[d],
            send_sem=send1,
            recv_sem=recv1.at[d],
            device_id=device(to),
            device_id_type=MESH,
        )

    def reply(d):
        to = lax.rem(me + peers - d, peers)
        return pltpu.make_async_remote_copy(
            src_ref=outbox.at[d],
            dst_ref=back.at[me],
            send_sem=send2,
            recv_sem=recv2,
            device_id=device(to),
            device_id_type=MESH,
        )

    def start(d, _):
        send(d).start()
        return 0

    columns_last(lat[...], lat_col)
    columns_last(count[...].astype(f32), count_col)
    scale_col[...] = jnp.broadcast_to(
        jnp.sum(
            jnp.where(iota((32, 32), 0) == iota((32, 32), 1), jnp.broadcast_to(scale[...], (32, 32)), 0.0),
            axis=1,
            keepdims=True,
        ),
        (32, 128),
    )
    acc[...] = jnp.zeros_like(acc)
    weights_of(left, right, stoich_t, w_a, w_b, s_both, s_high)
    load.wait()

    def gather(x, _):
        y_out[0, x] = st[x + 1, tile_y - 1 : tile_y, :]
        y_out[1, x] = st[x + 1, 0:1, :]
        return 0

    lax.fori_loop(0, tile_x, gather, 0, unroll=4)
    top_of(st[1 : tile_x + 1, :, 0:128].reshape(tile_x * tile_y, 128), top)
    pl.semaphore_wait(barrier, peers - 1)
    for n in range(4):
        pl.when(edges[n][3])(edge(n).start)
    lax.fori_loop(1, peers, start, 0)
    keep = pltpu.make_async_copy(msg.at[me], inbox.at[0], recv1.at[0])
    keep.start()

    for n in range(4):
        pl.when(edges[n][4])(edge(n).wait_recv)
    prepare(st, y_in, lat_col, count, diff, rhs, iface)
    for block in (0, 2):
        eliminate(rhs, coef, iface, scale_col, block)
    keep.wait()

    def work(c, first):
        for p in range(BATCH):
            if not (first and p == 0):
                send(c * BATCH + p).wait_recv()

        def put(p, value):
            outbox[pl.ds(c * BATCH + p, 1)] = value[None]

        flux_of([inbox[c * BATCH + p] for p in range(BATCH)], top, acc, put)
        for p in range(BATCH):
            if not (first and p == 0):
                reply(c * BATCH + p).start()

    work(0, True)

    def step(c, _):
        work(c, False)
        return 0

    lax.fori_loop(1, peers // BATCH, step, 0)
    own = pltpu.make_async_copy(outbox.at[0], back.at[me], recv1.at[0])
    own.start()
    whole = pltpu.make_async_copy(st.at[pl.ds(1, tile_x)], done, local.at[1])

    def columns(i, _):
        finish(rhs, coef, count_col, acc, w_a, w_b, s_both, s_high, solved_t, st, i)
        part = pl.ds(8 * i, 8)
        pltpu.make_async_copy(st.at[pl.ds(8 * i + 1, 8)], done.at[part], local.at[1]).start()
        return 0

    lax.fori_loop(0, tile_x // 8, columns, 0)
    whole.wait()
    own.wait()
    for n in range(4):
        pl.when(edges[n][3])(edge(n).wait_send)
    rest = pl.ds(0, peers - 1)
    pltpu.make_async_copy(msg.at[rest], msg.at[rest], send1).wait()
    pltpu.make_async_copy(outbox.at[rest], outbox.at[rest], send2).wait()
    pltpu.make_async_copy(back.at[rest], back.at[rest], recv2).wait()


def exchange(msg, state, lat, count, diffusion, scale, left, right, stoich_t):
    peers = msg.shape[0]
    tile_x, tile_y, width = state.shape
    return pl.pallas_call(
        exchange_kernel,
        out_shape=(
            jax.ShapeDtypeStruct((peers, ROWS, 128), f32),
            jax.ShapeDtypeStruct(state.shape, f32),
        ),
        in_specs=[ANY, ANY] + [VM] * 7,
        out_specs=(ANY, ANY),
        scratch_shapes=[
            pltpu.VMEM((tile_x + 2, tile_y, width), f32),
            pltpu.VMEM((2, tile_x, 1, width), f32),
            pltpu.VMEM((2, tile_x, 1, width), f32),
            pltpu.VMEM((4, width, 256), f32),
            pltpu.VMEM((4, width, 256), f32),
            pltpu.VMEM((4, 64, 256), f32),
            pltpu.VMEM((8, 32, 128), f32),
            pltpu.VMEM((8, 32, 128), f32),
            pltpu.VMEM((32, 128), f32),
            pltpu.VMEM((peers, MSG, 128), f32),
            pltpu.VMEM((peers, ROWS, 128), f32),
            pltpu.VMEM((256, 256), bf16),
            pltpu.VMEM((256, 256), f32),
            pltpu.VMEM((256, 256), bf16),
            pltpu.VMEM((256, 256), bf16),
            pltpu.VMEM((256, 256), bf16),
            pltpu.VMEM((256, 128), bf16),
            pltpu.VMEM((width, 256), f32),
            pltpu.SemaphoreType.DMA,
            pltpu.SemaphoreType.DMA((peers,)),
            pltpu.SemaphoreType.DMA,
            pltpu.SemaphoreType.DMA,
            pltpu.SemaphoreType.DMA((4,)),
            pltpu.SemaphoreType.DMA((4,)),
            pltpu.SemaphoreType.DMA((2,)),
        ],
        compiler_params=pltpu.CompilerParams(collective_id=0, has_side_effects=True, vmem_limit_bytes=58 << 20),
        name="exchange",
    )(msg, state, lat, count, diffusion, scale, left, right, stoich_t)


def unpack_kernel(flat, back, stream_t, done, out, state_out, buf, rows, held, sem):
    load = pltpu.make_async_copy(done, held, sem.at[0])
    store = pltpu.make_async_copy(held, state_out, sem.at[1])
    load.start()
    groups = flat.shape[0]
    peers = back.shape[0]

    def spread(t, _):
        m = back[pl.ds(pl.multiple_of(t * FORM, FORM), FORM)].reshape(FORM * 16, 128)
        parts = [m] + [pltpu.roll(m, 128 - 32 * q, axis=1) for q in range(1, 4)]
        parts = [p.reshape(FORM, 1, 16, 128) for p in parts]
        at = pl.multiple_of(t * FORM * CAP, FORM * CAP)
        buf[pl.ds(at, FORM * CAP), :] = jnp.concatenate(parts, axis=1).reshape(FORM * CAP, 128)
        return 0

    lax.fori_loop(0, peers // FORM, spread, 0)

    def move(g, _):
        at = pl.multiple_of(g * 128, 128)
        for j in range(128):
            rows[pl.ds(j, 1), :] = buf[pl.ds(flat[g, j], 1), :]
        out[:, pl.ds(at, 128)] = stream_t[:, pl.ds(at, 128)] - 0.5 * rows[...].T[0:32, :]
        return 0

    load.wait()
    store.start()
    lax.fori_loop(0, groups, move, 0)
    store.wait()


def unpack(flat, back, stream_t, done):
    peers = back.shape[0]
    return pl.pallas_call(
        unpack_kernel,
        out_shape=(jax.ShapeDtypeStruct(stream_t.shape, f32), jax.ShapeDtypeStruct(done.shape, f32)),
        in_specs=[pl.BlockSpec(memory_space=pltpu.SMEM), VM, VM, ANY],
        out_specs=(VM, ANY),
        scratch_shapes=[pltpu.VMEM((peers * CAP, 128), f32), pltpu.VMEM((128, 128), f32), pltpu.VMEM(done.shape, f32), pltpu.SemaphoreType.DMA((2,))],
        compiler_params=pltpu.CompilerParams(vmem_limit_bytes=48 << 20),
        name="unpack",
    )(flat, back, stream_t, done)


def body(
    state,
    lat_coef,
    diffusion,
    layer_count,
    species_scale,
    stream,
    reach_owner,
    reach_local,
    exch_coef,
    rate_left,
    rate_right,
    stoich,
):
    peers = lax.axis_size("gx") * lax.axis_size("gy")
    stream_t = stream.T
    flat, msg = pack(
        reach_owner.reshape(-1, 128), reach_local.reshape(-1, 128), exch_coef.reshape(-1, 128), stream_t, peers
    )
    back, done = exchange(
        msg, state, lat_coef, layer_count, diffusion, species_scale[None, :], rate_left, rate_right, stoich.T
    )
    stream_out, state_out = unpack(flat, back, stream_t, done)
    return (state_out, stream_out.T)


def solution(mesh):
    return jax.shard_map(
        body,
        mesh=mesh,
        in_specs=(
            P("gx", "gy", None),
            P("gx", "gy"),
            P("gx", "gy", None),
            P("gx", "gy"),
            P(),
            P(("gx", "gy"), None),
            P(("gx", "gy"), None),
            P(("gx", "gy")),
            P(("gx", "gy")),
            P(),
            P(),
            P(),
        ),
        out_specs=(P("gx", "gy", None), P(("gx", "gy"), None)),
        check_vma=False,
    )
```

```python
import functools

import jax
import jax.numpy as jnp
from jax import lax
from jax.experimental import pallas as pl
from jax.experimental.pallas import tpu as pltpu
from jax.sharding import PartitionSpec as P

MESH = pl.DeviceIdType.MESH
f32, bf16, i32 = jnp.float32, jnp.bfloat16, jnp.int32
VM = pl.BlockSpec(memory_space=pltpu.VMEM)
ANY = pl.BlockSpec(memory_space=pl.ANY)

CAP = 64
ROWS = 16
MSG = ROWS + 1
FORM = 32
BATCH = 16
STRIDE = 45


def iota(shape, dim):
    return lax.broadcasted_iota(i32, shape, dim)


def split(x):
    hi = x.astype(bf16)
    return hi, (x - hi.astype(f32)).astype(bf16)


def dot(a, b):
    return jnp.dot(a, b, preferred_element_type=f32)


def pack_kernel(
    owner_in, local_in, coef_in, stream_in, flat_out, msg_out,
    owner, local, coef, stream_t, msg, rows, buf, flat_v, flat_s, sem,
):
    groups = owner.shape[0]
    peers = msg.shape[0]
    inputs = ((owner_in, owner), (local_in, local), (coef_in, coef), (stream_in, stream_t))
    loads = [pltpu.make_async_copy(a, b, sem.at[n]) for n, (a, b) in enumerate(inputs)]
    for load in loads:
        load.start()
    sub, lane = iota((128, 128), 0), iota((128, 128), 1)
    upto = (sub <= lane).astype(bf16)
    ones = jnp.ones((128, 128), bf16)
    carry = jnp.zeros((128, 128), f32)
    loads[0].wait()
    for g in range(groups):
        mine = sub == owner[g : g + 1, :]
        onehot = mine.astype(f32).astype(bf16)
        count = dot(onehot, upto) + carry
        carry = carry + dot(onehot, ones)
        rank = jnp.sum(jnp.where(mine, count, 0.0), axis=0, keepdims=True)
        flat_v[g : g + 1, :] = owner[g : g + 1, :] * CAP + rank.astype(i32) - 1
    flat_copy = pltpu.make_async_copy(flat_v, flat_s, sem.at[4])
    flat_copy.start()
    flat_out[...] = flat_v[...]
    for load in loads[1:]:
        load.wait()

    def fill(g, _):
        at = pl.multiple_of(g * 128, 128)
        block = jnp.concatenate(
            [
                stream_t[:, pl.ds(at, 128)],
                local[pl.ds(g, 1), :].astype(f32),
                coef[pl.ds(g, 1), :],
                jnp.zeros((94, 128), f32),
            ],
            axis=0,
        )
        rows[pl.ds(at, 128), :] = block.T
        return 0

    lax.fori_loop(0, groups, fill, 0, unroll=4)
    empty = jnp.where(lane == 32, -1.0, 0.0)

    def clear(g, _):
        buf[pl.ds(pl.multiple_of(g * 128, 128), 128), :] = empty
        return 0

    lax.fori_loop(0, buf.shape[0] // 128, clear, 0, unroll=4)
    flat_copy.wait()

    def move(g, _):
        for j in range(128):
            buf[pl.ds(flat_s[g, j], 1), :] = rows[pl.ds(g * 128 + j, 1), :]
        return 0

    lax.fori_loop(0, groups, move, 0)
    lanes = iota((FORM * 16, 128), 1)
    group, pair = lanes // 32, lanes % 32 < 2
    spot = lanes // 8 == (16 - iota((FORM * 16, 128), 0) % 16) % 16

    def form(t, _):
        at = pl.multiple_of(t * FORM * CAP, FORM * CAP)
        part = buf[pl.ds(at, FORM * CAP), :].reshape(FORM, 4, 16, 128)
        part = [part[:, q].reshape(FORM * 16, 128) for q in range(4)]
        part = [part[0]] + [pltpu.roll(part[q], 32 * q, axis=1) for q in range(1, 4)]
        vals = part[3]
        for q in (2, 1, 0):
            vals = jnp.where(group == q, part[q], vals)
        even = jnp.where(pair & (group == 1), part[0], 0.0) + jnp.where(pair & (group == 3), part[2], 0.0)
        odd = jnp.where(pair & (group == 2), part[1], 0.0) + jnp.where(pair & (group == 0), part[3], 0.0)
        meta = even + pltpu.roll(odd, 98, axis=1)
        meta = jnp.where(group == 1, meta, 0.0) + pltpu.roll(jnp.where(group == 3, meta, 0.0), 68, axis=1)
        for shift in (8, 16, 32, 64):
            meta = meta + pltpu.roll(meta, shift, axis=1)
        meta = jnp.sum(jnp.where(spot, meta, 0.0).reshape(FORM, 16, 128), axis=1)
        to = pl.ds(pl.multiple_of(t * FORM, FORM), FORM)
        msg[to, pl.ds(0, ROWS), :] = vals.reshape(FORM, 16, 128)
        msg[to, pl.ds(ROWS, 1), :] = meta[:, None, :]
        pltpu.make_async_copy(msg.at[to], msg_out.at[to], sem.at[5]).start()
        return 0

    lax.fori_loop(0, peers // FORM, form, 0)
    pltpu.make_async_copy(msg, msg_out, sem.at[5]).wait()


def pack(owner, local, coef, stream_t, peers):
    groups = owner.shape[0]
    return pl.pallas_call(
        pack_kernel,
        out_shape=(
            jax.ShapeDtypeStruct((groups, 128), i32),
            jax.ShapeDtypeStruct((peers, MSG, 128), f32),
        ),
        in_specs=[ANY] * 4,
        out_specs=(VM, ANY),
        scratch_shapes=[
            pltpu.VMEM(owner.shape, i32),
            pltpu.VMEM(local.shape, i32),
            pltpu.VMEM(coef.shape, f32),
            pltpu.VMEM(stream_t.shape, f32),
            pltpu.VMEM((peers, MSG, 128), f32),
            pltpu.VMEM((groups * 128, 128), f32),
            pltpu.VMEM((peers * CAP, 128), f32),
            pltpu.VMEM((groups, 128), i32),
            pltpu.SMEM((groups, 128), i32),
            pltpu.SemaphoreType.DMA((6,)),
        ],
        compiler_params=pltpu.CompilerParams(vmem_limit_bytes=60 << 20),
        name="pack",
    )(owner, local, coef, stream_t)


def flux_of(messages, top, acc, put):
    count = len(messages)
    rows = count * ROWS
    lane = iota((rows, 128), 1)
    lane_f, place, side = lane.astype(f32), lane // 32, (lane // 64).astype(f32)
    vals = jnp.concatenate([m[0:ROWS, :] for m in messages], axis=0)
    meta = jnp.concatenate(
        [
            pltpu.roll(jnp.broadcast_to(m[ROWS : ROWS + 1, :], (ROWS, 128)), 0, axis=1, stride=8, stride_axis=0)
            for m in messages
        ],
        axis=0,
    )

    def by_place(parts):
        out = parts[3]
        for q in (2, 1, 0):
            out = jnp.where(place == q, parts[q], out)
        return out

    onehots, parts, coefs = [], [], []
    for q in range(4):
        column = jnp.broadcast_to(meta[:, 2 * q : 2 * q + 1], (rows, 128))
        part = jnp.floor(column * (1.0 / 256.0))
        low = column - 256.0 * part
        onehots.append(
            jnp.concatenate(
                [jnp.where(low == lane_f + 128.0 * b, 1.0, 0.0).astype(bf16) for b in range(2)], axis=1
            )
        )
        parts.append(part)
        coefs.append(jnp.broadcast_to(meta[:, 2 * q + 1 : 2 * q + 2], (rows, 128)))
    onehot = jnp.concatenate(onehots, axis=0)
    picked = dot(onehot, top[...])
    tops = []
    for q in range(4):
        p = picked[rows * q : rows * q + rows, :]
        p = jnp.where(parts[q] == side, p[:, 0:128], 0.0) + jnp.where(parts[q] == side + 2.0, p[:, 128:256], 0.0)
        p = p + pltpu.roll(p, 64, axis=1)
        tops.append(p + pltpu.roll(p, 32, axis=1))
    flux = by_place(coefs) * (vals - by_place(tops))
    for p in range(count):
        put(p, flux[ROWS * p : ROWS * p + ROWS, :])
    flux_t, part_t = flux.T, by_place(parts).T
    flux_t = jnp.concatenate([flux_t[32 * q : 32 * q + 32, :] for q in range(4)], axis=1)
    part_t = jnp.concatenate([part_t[32 * q : 32 * q + 1, :] for q in range(4)], axis=1)
    high = flux_t.astype(bf16).astype(f32)
    both = jnp.concatenate([high, flux_t - high], axis=0)
    spread = jnp.concatenate([jnp.where(part_t == float(g), both, 0.0).astype(bf16) for g in range(4)], axis=0)
    acc[...] += dot(spread, onehot)


def top_of(state_top, top):
    lane = iota((256, 128), 1)
    quarters = []
    for g in range(4):
        t = jnp.where(lane < 32, state_top[256 * g : 256 * g + 256, :], 0.0)
        high = t.astype(bf16).astype(f32)
        quarters.append(high + pltpu.roll(t - high, 32, axis=1))
    top[...] = jnp.concatenate(
        [quarters[g] + pltpu.roll(quarters[g + 1], 64, axis=1) for g in (0, 2)], axis=1
    ).astype(bf16)


def prepare(st, y_in, lat_col, rhs):
    row = iota((32, 128), 0)

    def step(cb, _):
        block, lanes = cb // 2, pl.ds(pl.multiple_of(lax.rem(cb, 2) * 128, 128), 128)
        lats = [jnp.broadcast_to(lat_col[cb, :, x : x + 1], (32, 128)) for x in range(4)]
        for j in range(16):
            at = slice(128 * j, 128 * j + 128)
            parts = []
            for x in range(4):
                here = 4 * cb + x
                s = st[here + 1, :, at]
                lower = jnp.where(row == 0, y_in[0, here, :, at], pltpu.roll(s, 1, axis=0))
                upper = jnp.where(row == 31, y_in[1, here, :, at], pltpu.roll(s, 31, axis=0))
                beside = (st[here, :, at] + st[here + 2, :, at]) + (lower + upper)
                parts.append(s + lats[x] * (beside - 4.0 * s))
            rhs[block, at, lanes] = jnp.concatenate(parts, axis=0).T
        return 0

    lax.fori_loop(0, 8, step, 0)


def sizes_of(diff, count, iface):
    for cb in range(8):
        counts = jnp.concatenate([count[4 * cb + x : 4 * cb + x + 1, :] for x in range(4)], axis=1)
        d = diff[4 * cb : 4 * cb + 4].reshape(128, 64)
        d = jnp.concatenate([d, jnp.zeros((128, 64), f32)], axis=1).T[0:64, :]
        lanes = slice(128 * (cb % 2), 128 * (cb % 2) + 128)
        iface[cb // 2, :, lanes] = jnp.where(iota((64, 128), 0) + 1 < counts, d, 0.0)


def cell(k):
    return pl.ds(32 * k, 32)


def put2(ref, block, k, value):
    ref[block, cell(k), :] = value[:, 0:256]
    ref[block + 1, cell(k), :] = value[:, 256:512]


def get2(ref, block, k):
    return jnp.concatenate([ref[block, cell(k), :], ref[block + 1, cell(k), :]], axis=1)


def below(iface, scale_col, block, k):
    row = jnp.concatenate([iface[block, pl.ds(k, 1), :], iface[block + 1, pl.ds(k, 1), :]], axis=1)
    return jnp.concatenate([scale_col[...]] * 4, axis=1) * row


def factor(coef, pivot, iface, scale_col, block, n, carry):
    c, u = carry
    for m in range(7):
        k = 63 - 7 * n - m
        v = below(iface, scale_col, block, k - 1)
        r = 1.0 / (1.0 + v + u * (1.0 - c))
        c = v * r
        u = v
        put2(coef, block, k, c)
        put2(pivot, block, k, r)
    return c, u


def factor_top(coef, block, carry):
    c, u = carry
    put2(coef, block, 0, 1.0 / (1.0 + u * (1.0 - c)))


def eliminate(rhs, coef, pivot, iface, scale_col, block):
    def layers(n, carry):
        d, u = carry
        for m in range(7):
            k = 63 - 7 * n - m
            d = (get2(rhs, block, k) + u * d) * get2(pivot, block, k)
            u = below(iface, scale_col, block, k - 1)
            put2(rhs, block, k, d)
        return d, u

    zero = jnp.zeros((32, 512), f32)
    d, u = lax.fori_loop(0, 9, layers, (zero, zero))
    put2(rhs, block, 0, (get2(rhs, block, 0) + u * d) * get2(coef, block, 0))


PART = 8


def columns_last(a, out):
    a = jnp.concatenate([a, jnp.zeros((32, 96), f32)], axis=1)
    a = jnp.concatenate([a, jnp.zeros((96, 128), f32)], axis=0).T
    for g in range(8):
        out[g] = pltpu.roll(a, (128 - 4 * g) % 128, axis=1)[0:32, :]


def weights_of(left, right, stoich_t, w_a, w_b, s_both, s_high):
    inside = iota((64, 128), 0) // 32 == iota((64, 128), 1) // 64

    def spread(w):
        return jnp.where(inside, jnp.concatenate([jnp.concatenate([w] * 2, axis=1)] * 2, axis=0), 0.0)

    pair = jnp.concatenate([spread(left[...]), spread(right[...])], axis=1)
    high, low = split(pair)
    none = jnp.zeros((64, 256), bf16)
    w_a[...] = jnp.concatenate([high, high, low, none], axis=0)
    w_b[...] = jnp.concatenate([high, high, none, low], axis=0)
    inside = iota((128, 256), 0) // 32 == iota((128, 256), 1) // 64
    wide = jnp.concatenate([stoich_t[...]] * 4, axis=1)
    high, low = split(jnp.where(inside, jnp.concatenate([wide] * 4, axis=0), 0.0).T)
    s_both[...] = jnp.concatenate([high, low], axis=1)
    s_high[...] = high


def finish(rhs, coef, count_col, acc, w_a, w_b, s_both, s_high, solved_t, st, i):
    lane = iota((128, 128), 1)
    at = pl.multiple_of(64 * i, 64)
    source = acc[pl.ds(at, 32), :] + acc[pl.ds(at + 32, 32), :]
    x = rhs[i, 0:32, :] + coef[i, 0:32, :] * source
    solved_t[0:32, :] = x
    for k in range(1, 64):
        cell = slice(32 * k, 32 * k + 32)
        x = rhs[i, cell, :] + coef[i, cell, :] * x
        solved_t[cell, :] = x

    half = lane < 64
    for cb in range(2):
        counts = jnp.concatenate(
            [jnp.broadcast_to(count_col[2 * i + cb, :, x : x + 1], (32, 128)) for x in range(4)], axis=0
        )
        depth = counts - (lane // 32).astype(f32)
        for first in range(0, 16, PART):
            solved, pair_a, pair_b = [], [], []
            for j in range(first, first + PART):
                x = solved_t[128 * j : 128 * j + 128, 128 * cb : 128 * cb + 128].T
                high = x.astype(bf16)
                wide = high.astype(f32)
                low = pltpu.roll(x - wide, 64, axis=1)
                pair_a.append(jnp.concatenate([jnp.where(half, wide, low).astype(bf16), high], axis=1))
                pair_b.append(jnp.concatenate([jnp.where(half, low, wide).astype(bf16), high], axis=1))
                solved.append(x)
            both = dot(jnp.concatenate(pair_a, axis=0), w_a[...])
            rates_a = split(both[:, 0:128] * both[:, 128:256])
            both = dot(jnp.concatenate(pair_b, axis=0), w_b[...])
            rates_b = split(both[:, 0:128] * both[:, 128:256])
            change = dot(jnp.concatenate([rates_a[0], rates_b[0]], axis=1), s_both[...])
            change = change[:, 0:128] + change[:, 128:256]
            change = change + dot(jnp.concatenate([rates_a[1], rates_b[1]], axis=1), s_high[...])
            for n in range(PART):
                j = first + n
                new = solved[n] + jnp.where(depth > 4.0 * j, 0.1, 0.0) * change[128 * n : 128 * n + 128, :]
                for p in range(4):
                    st[8 * i + 4 * cb + p + 1, :, 128 * j : 128 * j + 128] = new[32 * p : 32 * p + 32, :]


def exchange_kernel(
    msg, state, lat, count, diff, scale, left, right, stoich_t, back, done,
    st, y_in, y_out, rhs, coef, iface, lat_col, count_col, scale_col, inbox, outbox, top, acc,
    w_a, w_b, s_both, s_high, solved_t, pivot,
    send1, recv1, send2, recv2, send_edge, recv_edge, local,
):
    peers = msg.shape[0]
    size_x, size_y = lax.axis_size("gx"), lax.axis_size("gy")
    gx, gy = lax.axis_index("gx"), lax.axis_index("gy")
    me = gx * size_y + gy
    tile_x, tile_y, _ = state.shape

    def device(t):
        return (t // size_y, lax.rem(t, size_y))

    barrier = pltpu.get_barrier_semaphore()

    def greet(d, _):
        pl.semaphore_signal(barrier, inc=1, device_id=device(lax.rem(me + d, peers)), device_id_type=MESH)
        return 0

    lax.fori_loop(1, peers, greet, 0)
    load = pltpu.make_async_copy(state, st.at[pl.ds(1, tile_x)], local.at[0])
    load.start()

    edges = [
        (state.at[pl.ds(tile_x - 1, 1)], st.at[pl.ds(0, 1)], (lax.rem(gx + 1, size_x), gy), gx < size_x - 1, gx > 0),
        (state.at[pl.ds(0, 1)], st.at[pl.ds(tile_x + 1, 1)], (lax.rem(gx + size_x - 1, size_x), gy), gx > 0, gx < size_x - 1),
        (y_out.at[0], y_in.at[0], (gx, lax.rem(gy + 1, size_y)), gy < size_y - 1, gy > 0),
        (y_out.at[1], y_in.at[1], (gx, lax.rem(gy + size_y - 1, size_y)), gy > 0, gy < size_y - 1),
    ]

    def edge(n):
        block, to, device_id, _, _ = edges[n]
        return pltpu.make_async_remote_copy(
            src_ref=block,
            dst_ref=to,
            send_sem=send_edge.at[n],
            recv_sem=recv_edge.at[n],
            device_id=device_id,
            device_id_type=MESH,
        )

    for n in range(4):
        @pl.when(jnp.logical_not(edges[n][4]))
        def _():
            edges[n][1][...] = jnp.zeros(edges[n][1].shape, f32)

    def send(d):
        to = lax.rem(me + d * STRIDE, peers)
        return pltpu.make_async_remote_copy(
            src_ref=msg.at[to],
            dst_ref=inbox.at[d],
            send_sem=send1,
            recv_sem=recv1.at[d],
            device_id=device(to),
            device_id_type=MESH,
        )

    def reply(d):
        to = lax.rem(me + (peers - d) * STRIDE, peers)
        return pltpu.make_async_remote_copy(
            src_ref=outbox.at[d],
            dst_ref=back.at[me],
            send_sem=send2,
            recv_sem=recv2,
            device_id=device(to),
            device_id_type=MESH,
        )

    columns_last(lat[...], lat_col)
    columns_last(count[...].astype(f32), count_col)
    scale_col[...] = jnp.broadcast_to(
        jnp.sum(
            jnp.where(iota((32, 32), 0) == iota((32, 32), 1), jnp.broadcast_to(scale[...], (32, 32)), 0.0),
            axis=1,
            keepdims=True,
        ),
        (32, 128),
    )
    acc[...] = jnp.zeros_like(acc)
    weights_of(left, right, stoich_t, w_a, w_b, s_both, s_high)
    sizes_of(diff, count, iface)
    load.wait()

    def gather(x, _):
        y_out[0, x] = st[x + 1, tile_y - 1 : tile_y, :]
        y_out[1, x] = st[x + 1, 0:1, :]
        return 0

    lax.fori_loop(0, tile_x, gather, 0, unroll=4)
    top_of(st[1 : tile_x + 1, :, 0:128].reshape(tile_x * tile_y, 128), top)
    pl.semaphore_wait(barrier, peers - 1)
    for n in range(4):
        pl.when(edges[n][3])(edge(n).start)
    steps, zero = 9, jnp.zeros((32, 512), f32)
    each = (peers - 1) // (2 * steps)
    for half, block in enumerate((0, 2)):

        def start(n, carry, half=half, block=block):
            for m in range(each):
                send(1 + (half * steps + n) * each + m).start()
            return factor(coef, pivot, iface, scale_col, block, n, carry)

        factor_top(coef, block, lax.fori_loop(0, steps, start, (zero, zero)))
    for d in range(1 + 2 * steps * each, peers):
        send(d).start()
    keep = pltpu.make_async_copy(msg.at[me], inbox.at[0], recv1.at[0])
    keep.start()

    for n in range(4):
        pl.when(edges[n][4])(edge(n).wait_recv)
    prepare(st, y_in, lat_col, rhs)
    for block in (0, 2):
        eliminate(rhs, coef, pivot, iface, scale_col, block)
    keep.wait()

    def work(c, first):
        for p in range(BATCH):
            if not (first and p == 0):
                send(c * BATCH + p).wait_recv()

        def put(p, value):
            outbox[pl.ds(c * BATCH + p, 1)] = value[None]

        flux_of([inbox[c * BATCH + p] for p in range(BATCH)], top, acc, put)
        for p in range(BATCH):
            if not (first and p == 0):
                reply(c * BATCH + p).start()

    work(0, True)

    def step(c, _):
        work(c, False)
        return 0

    lax.fori_loop(1, peers // BATCH, step, 0, unroll=7)
    own = pltpu.make_async_copy(outbox.at[0], back.at[me], recv1.at[0])
    own.start()
    whole = pltpu.make_async_copy(st.at[pl.ds(1, tile_x)], done, local.at[1])

    def columns(i, _):
        finish(rhs, coef, count_col, acc, w_a, w_b, s_both, s_high, solved_t, st, i)
        part = pl.ds(8 * i, 8)
        pltpu.make_async_copy(st.at[pl.ds(8 * i + 1, 8)], done.at[part], local.at[1]).start()
        return 0

    lax.fori_loop(0, tile_x // 8, columns, 0)
    whole.wait()
    own.wait()
    for n in range(4):
        pl.when(edges[n][3])(edge(n).wait_send)
    rest = pl.ds(0, peers - 1)
    pltpu.make_async_copy(msg.at[rest], msg.at[rest], send1).wait()
    pltpu.make_async_copy(outbox.at[rest], outbox.at[rest], send2).wait()
    pltpu.make_async_copy(back.at[rest], back.at[rest], recv2).wait()


def exchange(msg, state, lat, count, diffusion, scale, left, right, stoich_t):
    peers = msg.shape[0]
    tile_x, tile_y, width = state.shape
    return pl.pallas_call(
        exchange_kernel,
        out_shape=(
            jax.ShapeDtypeStruct((peers, ROWS, 128), f32),
            jax.ShapeDtypeStruct(state.shape, f32),
        ),
        in_specs=[ANY, ANY] + [VM] * 7,
        out_specs=(ANY, ANY),
        scratch_shapes=[
            pltpu.VMEM((tile_x + 2, tile_y, width), f32),
            pltpu.VMEM((2, tile_x, 1, width), f32),
            pltpu.VMEM((2, tile_x, 1, width), f32),
            pltpu.VMEM((4, width, 256), f32),
            pltpu.VMEM((4, width, 256), f32),
            pltpu.VMEM((4, 64, 256), f32),
            pltpu.VMEM((8, 32, 128), f32),
            pltpu.VMEM((8, 32, 128), f32),
            pltpu.VMEM((32, 128), f32),
            pltpu.VMEM((peers, MSG, 128), f32),
            pltpu.VMEM((peers, ROWS, 128), f32),
            pltpu.VMEM((256, 256), bf16),
            pltpu.VMEM((256, 256), f32),
            pltpu.VMEM((256, 256), bf16),
            pltpu.VMEM((256, 256), bf16),
            pltpu.VMEM((256, 256), bf16),
            pltpu.VMEM((256, 128), bf16),
            pltpu.VMEM((width, 256), f32),
            pltpu.VMEM((4, width, 256), f32),
            pltpu.SemaphoreType.DMA,
            pltpu.SemaphoreType.DMA((peers,)),
            pltpu.SemaphoreType.DMA,
            pltpu.SemaphoreType.DMA,
            pltpu.SemaphoreType.DMA((4,)),
            pltpu.SemaphoreType.DMA((4,)),
            pltpu.SemaphoreType.DMA((2,)),
        ],
        compiler_params=pltpu.CompilerParams(collective_id=0, has_side_effects=True, vmem_limit_bytes=60 << 20),
        name="exchange",
    )(msg, state, lat, count, diffusion, scale, left, right, stoich_t)


def unpack_kernel(flat, back_in, stream_in, done, out, state_out, back, stream_t, buf, rows, held, sem):
    load = pltpu.make_async_copy(done, held, sem.at[0])
    store = pltpu.make_async_copy(held, state_out, sem.at[1])
    load_back = pltpu.make_async_copy(back_in, back, sem.at[2])
    load_stream = pltpu.make_async_copy(stream_in, stream_t, sem.at[3])
    load_back.start()
    load_stream.start()
    load.start()
    groups = flat.shape[0]
    peers = back.shape[0]

    def spread(t, _):
        m = back[pl.ds(pl.multiple_of(t * FORM, FORM), FORM)].reshape(FORM * 16, 128)
        parts = [m] + [pltpu.roll(m, 128 - 32 * q, axis=1) for q in range(1, 4)]
        parts = [p.reshape(FORM, 1, 16, 128) for p in parts]
        at = pl.multiple_of(t * FORM * CAP, FORM * CAP)
        buf[pl.ds(at, FORM * CAP), :] = jnp.concatenate(parts, axis=1).reshape(FORM * CAP, 128)
        return 0

    load_back.wait()
    lax.fori_loop(0, peers // FORM, spread, 0)
    load_stream.wait()

    def move(g, _):
        at = pl.multiple_of(g * 128, 128)
        for j in range(128):
            rows[pl.ds(j, 1), :] = buf[pl.ds(flat[g, j], 1), :]
        out[:, pl.ds(at, 128)] = stream_t[:, pl.ds(at, 128)] - 0.5 * rows[...].T[0:32, :]
        return 0

    load.wait()
    store.start()
    lax.fori_loop(0, groups, move, 0)
    store.wait()


def unpack(flat, back, stream_t, done):
    peers = back.shape[0]
    return pl.pallas_call(
        unpack_kernel,
        out_shape=(jax.ShapeDtypeStruct(stream_t.shape, f32), jax.ShapeDtypeStruct(done.shape, f32)),
        in_specs=[pl.BlockSpec(memory_space=pltpu.SMEM), ANY, ANY, ANY],
        out_specs=(VM, ANY),
        scratch_shapes=[
            pltpu.VMEM(back.shape, f32),
            pltpu.VMEM(stream_t.shape, f32),
            pltpu.VMEM((peers * CAP, 128), f32),
            pltpu.VMEM((128, 128), f32),
            pltpu.VMEM(done.shape, f32),
            pltpu.SemaphoreType.DMA((4,)),
        ],
        compiler_params=pltpu.CompilerParams(vmem_limit_bytes=60 << 20),
        name="unpack",
    )(flat, back, stream_t, done)


def body(
    state,
    lat_coef,
    diffusion,
    layer_count,
    species_scale,
    stream,
    reach_owner,
    reach_local,
    exch_coef,
    rate_left,
    rate_right,
    stoich,
):
    peers = lax.axis_size("gx") * lax.axis_size("gy")
    stream_t = stream.T
    flat, msg = pack(
        reach_owner.reshape(-1, 128), reach_local.reshape(-1, 128), exch_coef.reshape(-1, 128), stream_t, peers
    )
    back, done = exchange(
        msg, state, lat_coef, layer_count, diffusion, species_scale[None, :], rate_left, rate_right, stoich.T
    )
    stream_out, state_out = unpack(flat, back, stream_t, done)
    return (state_out, stream_out.T)


def solution(mesh):
    return jax.shard_map(
        body,
        mesh=mesh,
        in_specs=(
            P("gx", "gy", None),
            P("gx", "gy"),
            P("gx", "gy", None),
            P("gx", "gy"),
            P(),
            P(("gx", "gy"), None),
            P(("gx", "gy"), None),
            P(("gx", "gy")),
            P(("gx", "gy")),
            P(),
            P(),
            P(),
        ),
        out_specs=(P("gx", "gy", None), P(("gx", "gy"), None)),
        check_vma=False,
    )
```

```python
import functools

import jax
import jax.numpy as jnp
from jax import lax
from jax.experimental import pallas as pl
from jax.experimental.pallas import tpu as pltpu
from jax.sharding import PartitionSpec as P

MESH = pl.DeviceIdType.MESH
f32, bf16, i32 = jnp.float32, jnp.bfloat16, jnp.int32
VM = pl.BlockSpec(memory_space=pltpu.VMEM)
ANY = pl.BlockSpec(memory_space=pl.ANY)

CAP = 64
ROWS = 16
MSG = ROWS + 1
FORM = 32
TURN = 8
BATCH = 16
STRIDE = 45


def iota(shape, dim):
    return lax.broadcasted_iota(i32, shape, dim)


def split(x):
    hi = x.astype(bf16)
    return hi, (x - hi.astype(f32)).astype(bf16)


def dot(a, b):
    return jnp.dot(a, b, preferred_element_type=f32)


def pack_kernel(
    owner_in, local_in, coef_in, stream_in, flat_out, msg_out,
    owner, local, coef, stream_t, msg, rows, buf, flat_v, flat_s, sem,
):
    groups = owner.shape[0]
    peers = msg.shape[0]
    inputs = ((owner_in, owner), (local_in, local), (coef_in, coef), (stream_in, stream_t))
    loads = [pltpu.make_async_copy(a, b, sem.at[n]) for n, (a, b) in enumerate(inputs)]
    for load in loads:
        load.start()
    sub, lane = iota((128, 128), 0), iota((128, 128), 1)
    upto = (sub <= lane).astype(bf16)
    ones = jnp.ones((128, 128), bf16)
    carry = jnp.zeros((128, 128), f32)
    loads[0].wait()
    for g in range(groups):
        mine = sub == owner[g : g + 1, :]
        onehot = mine.astype(f32).astype(bf16)
        count = dot(onehot, upto) + carry
        carry = carry + dot(onehot, ones)
        rank = jnp.sum(jnp.where(mine, count, 0.0), axis=0, keepdims=True)
        flat_v[g : g + 1, :] = owner[g : g + 1, :] * CAP + rank.astype(i32) - 1
    flat_copy = pltpu.make_async_copy(flat_v, flat_s, sem.at[4])
    flat_copy.start()
    flat_out[...] = flat_v[...]
    for load in loads[1:]:
        load.wait()

    def fill(g, _):
        at = pl.multiple_of(g * 128, 128)
        block = jnp.concatenate(
            [
                stream_t[:, pl.ds(at, 128)],
                local[pl.ds(g, 1), :].astype(f32),
                coef[pl.ds(g, 1), :],
                jnp.zeros((94, 128), f32),
            ],
            axis=0,
        )
        rows[pl.ds(at, 128), :] = block.T
        return 0

    lax.fori_loop(0, groups, fill, 0, unroll=4)
    empty = jnp.where(lane == 32, -1.0, 0.0)

    def clear(g, _):
        buf[pl.ds(pl.multiple_of(g * 128, 128), 128), :] = empty
        return 0

    lax.fori_loop(0, buf.shape[0] // 128, clear, 0, unroll=4)
    flat_copy.wait()

    def move(g, _):
        for j in range(128):
            buf[pl.ds(flat_s[g, j], 1), :] = rows[pl.ds(g * 128 + j, 1), :]
        return 0

    lax.fori_loop(0, groups, move, 0)
    lanes = iota((FORM * 16, 128), 1)
    group, pair = lanes // 32, lanes % 32 < 2
    spot = lanes // 8 == (16 - iota((FORM * 16, 128), 0) % 16) % 16

    def form(t, _):
        at = pl.multiple_of(t * FORM * CAP, FORM * CAP)
        part = buf[pl.ds(at, FORM * CAP), :].reshape(FORM, 4, 16, 128)
        part = [part[:, q].reshape(FORM * 16, 128) for q in range(4)]
        part = [part[0]] + [pltpu.roll(part[q], 32 * q, axis=1) for q in range(1, 4)]
        vals = part[3]
        for q in (2, 1, 0):
            vals = jnp.where(group == q, part[q], vals)
        even = jnp.where(pair & (group == 1), part[0], 0.0) + jnp.where(pair & (group == 3), part[2], 0.0)
        odd = jnp.where(pair & (group == 2), part[1], 0.0) + jnp.where(pair & (group == 0), part[3], 0.0)
        meta = even + pltpu.roll(odd, 98, axis=1)
        meta = jnp.where(group == 1, meta, 0.0) + pltpu.roll(jnp.where(group == 3, meta, 0.0), 68, axis=1)
        for shift in (8, 16, 32, 64):
            meta = meta + pltpu.roll(meta, shift, axis=1)
        meta = jnp.sum(jnp.where(spot, meta, 0.0).reshape(FORM, 16, 128), axis=1)
        to = pl.ds(pl.multiple_of(t * FORM, FORM), FORM)
        msg[to, pl.ds(0, ROWS), :] = vals.reshape(FORM, 16, 128)
        msg[to, pl.ds(ROWS, 1), :] = meta[:, None, :]
        pltpu.make_async_copy(msg.at[to], msg_out.at[to], sem.at[5]).start()
        return 0

    lax.fori_loop(0, peers // FORM, form, 0)
    pltpu.make_async_copy(msg, msg_out, sem.at[5]).wait()


def pack(owner, local, coef, stream_t, peers):
    groups = owner.shape[0]
    return pl.pallas_call(
        pack_kernel,
        out_shape=(
            jax.ShapeDtypeStruct((groups, 128), i32),
            jax.ShapeDtypeStruct((peers, MSG, 128), f32),
        ),
        in_specs=[ANY] * 4,
        out_specs=(VM, ANY),
        scratch_shapes=[
            pltpu.VMEM(owner.shape, i32),
            pltpu.VMEM(local.shape, i32),
            pltpu.VMEM(coef.shape, f32),
            pltpu.VMEM(stream_t.shape, f32),
            pltpu.VMEM((peers, MSG, 128), f32),
            pltpu.VMEM((groups * 128, 128), f32),
            pltpu.VMEM((peers * CAP, 128), f32),
            pltpu.VMEM((groups, 128), i32),
            pltpu.SMEM((groups, 128), i32),
            pltpu.SemaphoreType.DMA((6,)),
        ],
        compiler_params=pltpu.CompilerParams(vmem_limit_bytes=60 << 20),
        name="pack",
    )(owner, local, coef, stream_t)


def flux_of(messages, top, acc, put):
    count = len(messages)
    rows = count * ROWS
    lane = iota((rows, 128), 1)
    lane_f, place, side = lane.astype(f32), lane // 32, (lane // 64).astype(f32)
    vals = jnp.concatenate([m[0:ROWS, :] for m in messages], axis=0)
    meta = jnp.concatenate(
        [
            pltpu.roll(jnp.broadcast_to(m[ROWS : ROWS + 1, :], (ROWS, 128)), 0, axis=1, stride=8, stride_axis=0)
            for m in messages
        ],
        axis=0,
    )

    def by_place(parts):
        out = parts[3]
        for q in (2, 1, 0):
            out = jnp.where(place == q, parts[q], out)
        return out

    onehots, parts, coefs = [], [], []
    for q in range(4):
        column = jnp.broadcast_to(meta[:, 2 * q : 2 * q + 1], (rows, 128))
        part = jnp.floor(column * (1.0 / 256.0))
        low = column - 256.0 * part
        onehots.append(
            jnp.concatenate(
                [jnp.where(low == lane_f + 128.0 * b, 1.0, 0.0).astype(bf16) for b in range(2)], axis=1
            )
        )
        parts.append(part)
        coefs.append(jnp.broadcast_to(meta[:, 2 * q + 1 : 2 * q + 2], (rows, 128)))
    onehot = jnp.concatenate(onehots, axis=0)
    picked = dot(onehot, top[...])
    tops = []
    for q in range(4):
        p = picked[rows * q : rows * q + rows, :]
        p = jnp.where(parts[q] == side, p[:, 0:128], 0.0) + jnp.where(parts[q] == side + 2.0, p[:, 128:256], 0.0)
        p = p + pltpu.roll(p, 64, axis=1)
        tops.append(p + pltpu.roll(p, 32, axis=1))
    flux = by_place(coefs) * (vals - by_place(tops))
    for p in range(count):
        put(p, flux[ROWS * p : ROWS * p + ROWS, :])
    flux_t, part_t = flux.T, by_place(parts).T
    flux_t = jnp.concatenate([flux_t[32 * q : 32 * q + 32, :] for q in range(4)], axis=1)
    part_t = jnp.concatenate([part_t[32 * q : 32 * q + 1, :] for q in range(4)], axis=1)
    high = flux_t.astype(bf16).astype(f32)
    both = jnp.concatenate([high, flux_t - high], axis=0)
    spread = jnp.concatenate([jnp.where(part_t == float(g), both, 0.0).astype(bf16) for g in range(4)], axis=0)
    acc[...] += dot(spread, onehot)


def top_of(state_top, top):
    lane = iota((256, 128), 1)
    quarters = []
    for g in range(4):
        t = jnp.where(lane < 32, state_top[256 * g : 256 * g + 256, :], 0.0)
        high = t.astype(bf16).astype(f32)
        quarters.append(high + pltpu.roll(t - high, 32, axis=1))
    top[...] = jnp.concatenate(
        [quarters[g] + pltpu.roll(quarters[g + 1], 64, axis=1) for g in (0, 2)], axis=1
    ).astype(bf16)


def prepare(st, y_in, lat_col, rhs):
    row = iota((32, 128), 0)

    def step(cb, _):
        block, lanes = cb // 2, pl.ds(pl.multiple_of(lax.rem(cb, 2) * 128, 128), 128)
        lats = [jnp.broadcast_to(lat_col[cb, :, x : x + 1], (32, 128)) for x in range(4)]
        for j in range(16):
            at = slice(128 * j, 128 * j + 128)
            parts = []
            for x in range(4):
                here = 4 * cb + x
                s = st[here + 1, :, at]
                lower = jnp.where(row == 0, y_in[0, here, :, at], pltpu.roll(s, 1, axis=0))
                upper = jnp.where(row == 31, y_in[1, here, :, at], pltpu.roll(s, 31, axis=0))
                beside = (st[here, :, at] + st[here + 2, :, at]) + (lower + upper)
                parts.append(s + lats[x] * (beside - 4.0 * s))
            rhs[block, at, lanes] = jnp.concatenate(parts, axis=0).T
        return 0

    lax.fori_loop(0, 8, step, 0)


def sizes_of(diff, count, iface):
    for cb in range(8):
        counts = jnp.concatenate([count[4 * cb + x : 4 * cb + x + 1, :] for x in range(4)], axis=1)
        d = diff[4 * cb : 4 * cb + 4].reshape(128, 64)
        d = jnp.concatenate([d, jnp.zeros((128, 64), f32)], axis=1).T[0:64, :]
        lanes = slice(128 * (cb % 2), 128 * (cb % 2) + 128)
        iface[cb // 2, :, lanes] = jnp.where(iota((64, 128), 0) + 1 < counts, d, 0.0)


def cell(k):
    return pl.ds(32 * k, 32)


def put2(ref, block, k, value):
    ref[block, cell(k), :] = value[:, 0:256]
    ref[block + 1, cell(k), :] = value[:, 256:512]


def get2(ref, block, k):
    return jnp.concatenate([ref[block, cell(k), :], ref[block + 1, cell(k), :]], axis=1)


def below(iface, scale_col, block, k):
    row = jnp.concatenate([iface[block, pl.ds(k, 1), :], iface[block + 1, pl.ds(k, 1), :]], axis=1)
    return jnp.concatenate([scale_col[...]] * 4, axis=1) * row


def factor(coef, pivot, iface, scale_col, block, n, carry):
    c, u = carry
    for m in range(7):
        k = 63 - 7 * n - m
        v = below(iface, scale_col, block, k - 1)
        r = 1.0 / (1.0 + v + u * (1.0 - c))
        c = v * r
        u = v
        put2(coef, block, k, c)
        put2(pivot, block, k, r)
    return c, u


def factor_top(coef, block, carry):
    c, u = carry
    put2(coef, block, 0, 1.0 / (1.0 + u * (1.0 - c)))


def eliminate(rhs, coef, pivot, iface, scale_col, block):
    def layers(n, carry):
        d, u = carry
        for m in range(7):
            k = 63 - 7 * n - m
            d = (get2(rhs, block, k) + u * d) * get2(pivot, block, k)
            u = below(iface, scale_col, block, k - 1)
            put2(rhs, block, k, d)
        return d, u

    zero = jnp.zeros((32, 512), f32)
    d, u = lax.fori_loop(0, 9, layers, (zero, zero))
    put2(rhs, block, 0, (get2(rhs, block, 0) + u * d) * get2(coef, block, 0))


PART = 8


def columns_last(a, out):
    a = jnp.concatenate([a, jnp.zeros((32, 96), f32)], axis=1)
    a = jnp.concatenate([a, jnp.zeros((96, 128), f32)], axis=0).T
    for g in range(8):
        out[g] = pltpu.roll(a, (128 - 4 * g) % 128, axis=1)[0:32, :]


def weights_of(left, right, stoich_t, w_a, w_b, s_both, s_high):
    inside = iota((64, 128), 0) // 32 == iota((64, 128), 1) // 64

    def spread(w):
        return jnp.where(inside, jnp.concatenate([jnp.concatenate([w] * 2, axis=1)] * 2, axis=0), 0.0)

    pair = jnp.concatenate([spread(left[...]), spread(right[...])], axis=1)
    high, low = split(pair)
    none = jnp.zeros((64, 256), bf16)
    w_a[...] = jnp.concatenate([high, high, low, none], axis=0)
    w_b[...] = jnp.concatenate([high, high, none, low], axis=0)
    inside = iota((128, 256), 0) // 32 == iota((128, 256), 1) // 64
    wide = jnp.concatenate([stoich_t[...]] * 4, axis=1)
    high, low = split(jnp.where(inside, jnp.concatenate([wide] * 4, axis=0), 0.0).T)
    s_both[...] = jnp.concatenate([high, low], axis=1)
    s_high[...] = high


def finish(rhs, coef, count_col, acc, w_a, w_b, s_both, s_high, solved_t, st, i):
    lane = iota((128, 128), 1)
    at = pl.multiple_of(64 * i, 64)
    source = acc[pl.ds(at, 32), :] + acc[pl.ds(at + 32, 32), :]
    x = rhs[i, 0:32, :] + coef[i, 0:32, :] * source
    solved_t[0:32, :] = x
    for k in range(1, 64):
        cell = slice(32 * k, 32 * k + 32)
        x = rhs[i, cell, :] + coef[i, cell, :] * x
        solved_t[cell, :] = x

    half = lane < 64
    for cb in range(2):
        counts = jnp.concatenate(
            [jnp.broadcast_to(count_col[2 * i + cb, :, x : x + 1], (32, 128)) for x in range(4)], axis=0
        )
        depth = counts - (lane // 32).astype(f32)
        for first in range(0, 16, PART):
            solved, pair_a, pair_b = [], [], []
            for j in range(first, first + PART):
                x = solved_t[128 * j : 128 * j + 128, 128 * cb : 128 * cb + 128].T
                high = x.astype(bf16)
                wide = high.astype(f32)
                low = pltpu.roll(x - wide, 64, axis=1)
                pair_a.append(jnp.concatenate([jnp.where(half, wide, low).astype(bf16), high], axis=1))
                pair_b.append(jnp.concatenate([jnp.where(half, low, wide).astype(bf16), high], axis=1))
                solved.append(x)
            both = dot(jnp.concatenate(pair_a, axis=0), w_a[...])
            rates_a = split(both[:, 0:128] * both[:, 128:256])
            both = dot(jnp.concatenate(pair_b, axis=0), w_b[...])
            rates_b = split(both[:, 0:128] * both[:, 128:256])
            change = dot(jnp.concatenate([rates_a[0], rates_b[0]], axis=1), s_both[...])
            change = change[:, 0:128] + change[:, 128:256]
            change = change + dot(jnp.concatenate([rates_a[1], rates_b[1]], axis=1), s_high[...])
            for n in range(PART):
                j = first + n
                new = solved[n] + jnp.where(depth > 4.0 * j, 0.1, 0.0) * change[128 * n : 128 * n + 128, :]
                for p in range(4):
                    st[8 * i + 4 * cb + p + 1, :, 128 * j : 128 * j + 128] = new[32 * p : 32 * p + 32, :]


def exchange_kernel(
    msg, state, lat, count, diff, scale, left, right, stoich_t, back, done,
    st, y_in, y_out, rhs, coef, iface, lat_col, count_col, scale_col, inbox, outbox, top, acc,
    w_a, w_b, s_both, s_high, solved_t, pivot,
    send1, recv1, send2, recv2, send_edge, recv_edge, local,
):
    peers = msg.shape[0]
    size_x, size_y = lax.axis_size("gx"), lax.axis_size("gy")
    gx, gy = lax.axis_index("gx"), lax.axis_index("gy")
    me = gx * size_y + gy
    tile_x, tile_y, _ = state.shape

    def device(t):
        return (t // size_y, lax.rem(t, size_y))

    barrier = pltpu.get_barrier_semaphore()

    def greet(d, _):
        pl.semaphore_signal(barrier, inc=1, device_id=device(lax.rem(me + d, peers)), device_id_type=MESH)
        return 0

    lax.fori_loop(1, peers, greet, 0)
    load = pltpu.make_async_copy(state, st.at[pl.ds(1, tile_x)], local.at[0])
    load.start()

    edges = [
        (state.at[pl.ds(tile_x - 1, 1)], st.at[pl.ds(0, 1)], (lax.rem(gx + 1, size_x), gy), gx < size_x - 1, gx > 0),
        (state.at[pl.ds(0, 1)], st.at[pl.ds(tile_x + 1, 1)], (lax.rem(gx + size_x - 1, size_x), gy), gx > 0, gx < size_x - 1),
        (y_out.at[0], y_in.at[0], (gx, lax.rem(gy + 1, size_y)), gy < size_y - 1, gy > 0),
        (y_out.at[1], y_in.at[1], (gx, lax.rem(gy + size_y - 1, size_y)), gy > 0, gy < size_y - 1),
    ]

    def edge(n):
        block, to, device_id, _, _ = edges[n]
        return pltpu.make_async_remote_copy(
            src_ref=block,
            dst_ref=to,
            send_sem=send_edge.at[n],
            recv_sem=recv_edge.at[n],
            device_id=device_id,
            device_id_type=MESH,
        )

    for n in range(4):
        @pl.when(jnp.logical_not(edges[n][4]))
        def _():
            edges[n][1][...] = jnp.zeros(edges[n][1].shape, f32)

    def send(d):
        to = lax.rem(me + d * STRIDE, peers)
        return pltpu.make_async_remote_copy(
            src_ref=msg.at[to],
            dst_ref=inbox.at[d],
            send_sem=send1,
            recv_sem=recv1.at[d],
            device_id=device(to),
            device_id_type=MESH,
        )

    def reply(d):
        to = lax.rem(me + (peers - d) * STRIDE, peers)
        return pltpu.make_async_remote_copy(
            src_ref=outbox.at[d],
            dst_ref=back.at[me],
            send_sem=send2,
            recv_sem=recv2,
            device_id=device(to),
            device_id_type=MESH,
        )

    columns_last(lat[...], lat_col)
    columns_last(count[...].astype(f32), count_col)
    scale_col[...] = jnp.broadcast_to(
        jnp.sum(
            jnp.where(iota((32, 32), 0) == iota((32, 32), 1), jnp.broadcast_to(scale[...], (32, 32)), 0.0),
            axis=1,
            keepdims=True,
        ),
        (32, 128),
    )
    acc[...] = jnp.zeros_like(acc)
    weights_of(left, right, stoich_t, w_a, w_b, s_both, s_high)
    sizes_of(diff, count, iface)
    load.wait()

    def gather(x, _):
        y_out[0, x] = st[x + 1, tile_y - 1 : tile_y, :]
        y_out[1, x] = st[x + 1, 0:1, :]
        return 0

    lax.fori_loop(0, tile_x, gather, 0, unroll=4)
    top_of(st[1 : tile_x + 1, :, 0:128].reshape(tile_x * tile_y, 128), top)
    pl.semaphore_wait(barrier, peers - 1)
    for n in range(4):
        pl.when(edges[n][3])(edge(n).start)
    steps, zero = 9, jnp.zeros((32, 512), f32)
    each = (peers - 1) // (2 * steps)
    for half, block in enumerate((0, 2)):

        def start(n, carry, half=half, block=block):
            for m in range(each):
                send(1 + (half * steps + n) * each + m).start()
            return factor(coef, pivot, iface, scale_col, block, n, carry)

        factor_top(coef, block, lax.fori_loop(0, steps, start, (zero, zero)))
    for d in range(1 + 2 * steps * each, peers):
        send(d).start()
    keep = pltpu.make_async_copy(msg.at[me], inbox.at[0], recv1.at[0])
    keep.start()

    for n in range(4):
        pl.when(edges[n][4])(edge(n).wait_recv)
    prepare(st, y_in, lat_col, rhs)
    for block in (0, 2):
        eliminate(rhs, coef, pivot, iface, scale_col, block)
    keep.wait()

    def work(c, first):
        for p in range(BATCH):
            if not (first and p == 0):
                send(c * BATCH + p).wait_recv()

        def put(p, value):
            outbox[pl.ds(c * BATCH + p, 1)] = value[None]

        flux_of([inbox[c * BATCH + p] for p in range(BATCH)], top, acc, put)
        for p in range(BATCH):
            if not (first and p == 0):
                reply(c * BATCH + p).start()

    work(0, True)

    def step(c, _):
        work(c, False)
        return 0

    lax.fori_loop(1, peers // BATCH, step, 0, unroll=7)
    own = pltpu.make_async_copy(outbox.at[0], back.at[me], recv1.at[0])
    own.start()
    whole = pltpu.make_async_copy(st.at[pl.ds(1, tile_x)], done, local.at[1])

    def columns(i, _):
        finish(rhs, coef, count_col, acc, w_a, w_b, s_both, s_high, solved_t, st, i)
        part = pl.ds(8 * i, 8)
        pltpu.make_async_copy(st.at[pl.ds(8 * i + 1, 8)], done.at[part], local.at[1]).start()
        return 0

    lax.fori_loop(0, tile_x // 8, columns, 0)
    whole.wait()
    own.wait()
    for n in range(4):
        pl.when(edges[n][3])(edge(n).wait_send)
    rest = pl.ds(0, peers - 1)
    pltpu.make_async_copy(msg.at[rest], msg.at[rest], send1).wait()
    pltpu.make_async_copy(outbox.at[rest], outbox.at[rest], send2).wait()
    pltpu.make_async_copy(back.at[rest], back.at[rest], recv2).wait()


def exchange(msg, state, lat, count, diffusion, scale, left, right, stoich_t):
    peers = msg.shape[0]
    tile_x, tile_y, width = state.shape
    return pl.pallas_call(
        exchange_kernel,
        out_shape=(
            jax.ShapeDtypeStruct((peers, ROWS, 128), f32),
            jax.ShapeDtypeStruct(state.shape, f32),
        ),
        in_specs=[ANY, ANY] + [VM] * 7,
        out_specs=(ANY, ANY),
        scratch_shapes=[
            pltpu.VMEM((tile_x + 2, tile_y, width), f32),
            pltpu.VMEM((2, tile_x, 1, width), f32),
            pltpu.VMEM((2, tile_x, 1, width), f32),
            pltpu.VMEM((4, width, 256), f32),
            pltpu.VMEM((4, width, 256), f32),
            pltpu.VMEM((4, 64, 256), f32),
            pltpu.VMEM((8, 32, 128), f32),
            pltpu.VMEM((8, 32, 128), f32),
            pltpu.VMEM((32, 128), f32),
            pltpu.VMEM((peers, MSG, 128), f32),
            pltpu.VMEM((peers, ROWS, 128), f32),
            pltpu.VMEM((256, 256), bf16),
            pltpu.VMEM((256, 256), f32),
            pltpu.VMEM((256, 256), bf16),
            pltpu.VMEM((256, 256), bf16),
            pltpu.VMEM((256, 256), bf16),
            pltpu.VMEM((256, 128), bf16),
            pltpu.VMEM((width, 256), f32),
            pltpu.VMEM((4, width, 256), f32),
            pltpu.SemaphoreType.DMA,
            pltpu.SemaphoreType.DMA((peers,)),
            pltpu.SemaphoreType.DMA,
            pltpu.SemaphoreType.DMA,
            pltpu.SemaphoreType.DMA((4,)),
            pltpu.SemaphoreType.DMA((4,)),
            pltpu.SemaphoreType.DMA((2,)),
        ],
        compiler_params=pltpu.CompilerParams(collective_id=0, has_side_effects=True, vmem_limit_bytes=60 << 20),
        name="exchange",
    )(msg, state, lat, count, diffusion, scale, left, right, stoich_t)


def unpack_kernel(flat, back_in, stream_in, done, out, state_out, back, stream_t, buf, rows, held, sem):
    load = pltpu.make_async_copy(done, held, sem.at[0])
    store = pltpu.make_async_copy(held, state_out, sem.at[1])
    load_back = pltpu.make_async_copy(back_in, back, sem.at[2])
    load_stream = pltpu.make_async_copy(stream_in, stream_t, sem.at[3])
    load_back.start()
    load_stream.start()
    load.start()
    groups = flat.shape[0]
    peers = back.shape[0]

    def spread(t, _):
        m = back[pl.ds(pl.multiple_of(t * FORM, FORM), FORM)].reshape(FORM * 16, 128)
        parts = [m] + [pltpu.roll(m, 128 - 32 * q, axis=1) for q in range(1, 4)]
        parts = [p.reshape(FORM, 1, 16, 128) for p in parts]
        at = pl.multiple_of(t * FORM * CAP, FORM * CAP)
        buf[pl.ds(at, FORM * CAP), :] = jnp.concatenate(parts, axis=1).reshape(FORM * CAP, 128)
        return 0

    load_back.wait()
    lax.fori_loop(0, peers // FORM, spread, 0)
    load_stream.wait()

    def move(g, _):
        for n in range(TURN):
            for j in range(128):
                rows[pl.ds(128 * n + j, 1), :] = buf[pl.ds(flat[TURN * g + n, j], 1), :]
        for n in range(TURN):
            at = pl.multiple_of((TURN * g + n) * 128, 128)
            out[:, pl.ds(at, 128)] = stream_t[:, pl.ds(at, 128)] - 0.5 * rows[128 * n : 128 * n + 128, :].T[0:32, :]
        return 0

    load.wait()
    store.start()
    lax.fori_loop(0, groups // TURN, move, 0)
    store.wait()


def unpack(flat, back, stream_t, done):
    peers = back.shape[0]
    return pl.pallas_call(
        unpack_kernel,
        out_shape=(jax.ShapeDtypeStruct(stream_t.shape, f32), jax.ShapeDtypeStruct(done.shape, f32)),
        in_specs=[pl.BlockSpec(memory_space=pltpu.SMEM), ANY, ANY, ANY],
        out_specs=(VM, ANY),
        scratch_shapes=[
            pltpu.VMEM(back.shape, f32),
            pltpu.VMEM(stream_t.shape, f32),
            pltpu.VMEM((peers * CAP, 128), f32),
            pltpu.VMEM((TURN * 128, 128), f32),
            pltpu.VMEM(done.shape, f32),
            pltpu.SemaphoreType.DMA((4,)),
        ],
        compiler_params=pltpu.CompilerParams(vmem_limit_bytes=60 << 20),
        name="unpack",
    )(flat, back, stream_t, done)


def body(
    state,
    lat_coef,
    diffusion,
    layer_count,
    species_scale,
    stream,
    reach_owner,
    reach_local,
    exch_coef,
    rate_left,
    rate_right,
    stoich,
):
    peers = lax.axis_size("gx") * lax.axis_size("gy")
    stream_t = stream.T
    flat, msg = pack(
        reach_owner.reshape(-1, 128), reach_local.reshape(-1, 128), exch_coef.reshape(-1, 128), stream_t, peers
    )
    back, done = exchange(
        msg, state, lat_coef, layer_count, diffusion, species_scale[None, :], rate_left, rate_right, stoich.T
    )
    stream_out, state_out = unpack(flat, back, stream_t, done)
    return (state_out, stream_out.T)


def solution(mesh):
    return jax.shard_map(
        body,
        mesh=mesh,
        in_specs=(
            P("gx", "gy", None),
            P("gx", "gy"),
            P("gx", "gy", None),
            P("gx", "gy"),
            P(),
            P(("gx", "gy"), None),
            P(("gx", "gy"), None),
            P(("gx", "gy")),
            P(("gx", "gy")),
            P(),
            P(),
            P(),
        ),
        out_specs=(P("gx", "gy", None), P(("gx", "gy"), None)),
        check_vma=False,
    )
```
